512 devices in a mesh: dp: 4 (over x_hi, core), head: 8 (over y), ctx: 16 (over z, x_lo).
Axes of the slice: x: 4 (x_hi: 2, x_lo: 2; x = x_hi * 2 + x_lo), y: 8, z: 8, core: 2. Of those that a mesh axis runs over, the one named last changes fastest.
Arguments:
- queries: bfloat16 [8192, 64, 128], P(('dp', 'ctx'), 'head'), parts along dimension 0, may hold values from -8 to 8
- keys: bfloat16 [8192, 8, 128], P(('dp', 'ctx'), 'head'), parts along dimension 0, may hold values from -5 to 5
- values: bfloat16 [8192, 8, 128], P(('dp', 'ctx'), 'head'), parts along dimension 0, may hold values from -6 to 6
- output_gradient: bfloat16 [8192, 64, 128], P(('dp', 'ctx'), 'head'), parts along dimension 0, may hold values from -6 to 6
- block_order: int32 [128], P('dp'), parts along dimension 0, may hold values from 0 to 31, each once
Outputs:
- attn_out: bfloat16 [8192, 64, 128], P(('dp', 'ctx'), 'head'), parts along dimension 0
- grad_queries: bfloat16 [8192, 64, 128], P(('dp', 'ctx'), 'head'), parts along dimension 0
- grad_keys: bfloat16 [8192, 8, 128], P(('dp', 'ctx'), 'head'), parts along dimension 0
- grad_values: bfloat16 [8192, 8, 128], P(('dp', 'ctx'), 'head'), parts along dimension 0
The draws below stay inside these ranges and needn't reach their ends.
There are 4 independent parts, one for each index of `dp`. The reference program is written for one: setup_inputs(seed, part) draws one part's arguments, and reference() takes and returns one part's arrays. A program takes and returns all parts, laid end to end along the dimension named above; each array names one. Nothing has to cross between parts.
Inputs may be any that keep to these rules, and one draw needn't show every extreme that they name: `block_order`: each of the 32 places occurs once.
All inputs are finite; a program needn't handle non-finite values.
Results may differ from the reference program's by a relative error of at most 0.035.
Values may be sent and summed in bfloat16 or wider, within the bound.
No kernel may reach another device: no remote copies, remote signals or barrier semaphores. Data moves between devices by JAX's collectives and lax.ppermute only.
A program may use at most 64 MiB of HBM per device.

```python
import math
import jax
import jax.numpy as jnp
from jax import lax

HEAD_SIZE = 128
QUERY_HEADS = 64
KEY_VALUE_HEADS = 8
DOCUMENT_TOKENS = 2048
BLOCK = 64
NBLK = 32


def drawn_rows():
    row_ids = jnp.arange(DOCUMENT_TOKENS, dtype=jnp.int32)
    return (row_ids % BLOCK == BLOCK // 2) & (row_ids // BLOCK % 4 == 1)


def shared_keys(key):
    part_list = jax.random.split(jax.random.fold_in(key, 101), 1)
    array_shape = (DOCUMENT_TOKENS, KEY_VALUE_HEADS, HEAD_SIZE)
    normal_part = jax.random.truncated_normal(part_list[0], -5.0, 5.0, array_shape, jnp.float32)
    base = normal_part
    chosen = drawn_rows()
    before = jnp.roll(chosen, -1)
    made = jnp.where(chosen[:, None, None], base, base)
    made = jnp.where(before[:, None, None], base, made)
    return made


def draw_keys(key, part):
    made = shared_keys(key)
    return made.astype(jnp.bfloat16)


def draw_queries(key, part):
    key = jax.random.fold_in(key, 7)
    part_list = jax.random.split(key, 1)
    array_shape = (DOCUMENT_TOKENS, QUERY_HEADS, HEAD_SIZE)
    normal_part = 2.0 * jax.random.truncated_normal(part_list[0], -4.0, 4.0, array_shape, jnp.float32)
    base = normal_part
    chosen = drawn_rows()[:, None, None]
    result = jnp.where(chosen, base, base)
    return result.astype(jnp.bfloat16)


def levels(stream_key, shape, cuts, least, largest):
    factor_of = 1.0
    for dim, blocks in cuts:
        steps = jax.random.uniform(jax.random.fold_in(jax.random.fold_in(stream_key, 6), dim), (blocks,), jnp.float32, least / len(cuts), largest / len(cuts))
        factor_of = factor_of * jnp.repeat(jnp.exp(steps), shape[dim] // blocks).reshape((-1,) + (1,) * (len(shape) - 1 - dim))
    return factor_of


def scatter_about(key, shape, deviation, most, cuts=(), kind=jnp.bfloat16):
    array = deviation * jax.random.normal(key, shape, jnp.float32)
    if cuts:
        array = array * levels(key, shape, cuts, -0.22, 0.18)
    return jnp.clip(array, -most, most).astype(kind)


def setup_inputs(seed: int = 0, part: int = 0) -> dict:
    arg_keys = jax.random.split(jax.random.key(seed), 6)
    own_keys = jax.random.split(jax.random.fold_in(arg_keys[5], part), 6)
    queries = draw_queries(jax.random.fold_in(jax.random.fold_in(arg_keys[5], part), 71), part)
    keys = draw_keys(jax.random.fold_in(jax.random.fold_in(arg_keys[5], part), 71), part)
    values = scatter_about(own_keys[2], (DOCUMENT_TOKENS, KEY_VALUE_HEADS, HEAD_SIZE), 1.0, 6.0, ((0, 16), (1, 8)))
    output_gradient = scatter_about(own_keys[3], (DOCUMENT_TOKENS, QUERY_HEADS, HEAD_SIZE), 1.0, 6.0, ((0, 16), (1, 8)))
    block_order = jax.random.permutation(own_keys[4], NBLK).astype(jnp.int32)
    return {"queries": queries, "keys": keys, "values": values, "output_gradient": output_gradient, "block_order": block_order}


def reference(queries, keys, values, output_gradient, block_order):
    repeat_count = QUERY_HEADS // KEY_VALUE_HEADS
    score_scale = 1.0 / math.sqrt(HEAD_SIZE)
    row_ids = jnp.arange(DOCUMENT_TOKENS, dtype=jnp.int32)
    places = block_order[row_ids // BLOCK] * BLOCK + row_ids % BLOCK
    visible = (places[None, :] <= places[:, None])[None, :, :]
    grouped_queries = jnp.transpose(queries.reshape(DOCUMENT_TOKENS, KEY_VALUE_HEADS, repeat_count, HEAD_SIZE), (1, 2, 0, 3))
    gradient_groups = jnp.transpose(output_gradient.reshape(DOCUMENT_TOKENS, KEY_VALUE_HEADS, repeat_count, HEAD_SIZE), (1, 2, 0, 3))
    key_groups = jnp.transpose(keys, (1, 0, 2))
    value_groups = jnp.transpose(values, (1, 0, 2))
    highest = lax.Precision.HIGHEST

    def one_group(operands):
        query_part = operands[0].astype(jnp.float32)
        key_part = operands[1].astype(jnp.float32)
        value_part = operands[2].astype(jnp.float32)
        grad_part = operands[3].astype(jnp.float32)
        scores = jnp.einsum('rte,ue->rtu', query_part, key_part, precision=highest) * score_scale
        masked = jnp.where(visible, scores, -jnp.inf)
        row_max = lax.optimization_barrier(jnp.max(masked, axis=-1))
        expo = jnp.exp(masked - row_max[..., None])
        row_sum = lax.optimization_barrier(jnp.sum(expo, axis=-1))
        weights_half = expo.astype(jnp.bfloat16)
        weights_half = lax.optimization_barrier(weights_half).astype(jnp.float32)
        attn = jnp.einsum('rtu,ue->rte', weights_half, value_part, precision=highest) / row_sum[..., None]
        attn = attn.astype(jnp.bfloat16)
        log_total = row_max + jnp.log(row_sum)
        row_delta = lax.optimization_barrier(jnp.sum(attn.astype(jnp.float32) * grad_part, axis=-1))
        probs = jnp.exp(masked - log_total[..., None])
        grad_probs = jnp.einsum('rte,ue->rtu', grad_part, value_part, precision=highest)
        grad_scores = probs * (grad_probs - row_delta[..., None])
        probs_half = lax.optimization_barrier(probs.astype(jnp.bfloat16)).astype(jnp.float32)
        grad_half = lax.optimization_barrier(grad_scores.astype(jnp.bfloat16)).astype(jnp.float32)
        grad_value = jnp.einsum('rtu,rte->ue', probs_half, grad_part, precision=highest)
        grad_key = jnp.einsum('rtu,rte->ue', grad_half, query_part, precision=highest) * score_scale
        grad_query = jnp.einsum('rtu,ue->rte', grad_half, key_part, precision=highest) * score_scale
        return (attn, grad_query.astype(jnp.bfloat16), grad_key.astype(jnp.bfloat16), grad_value.astype(jnp.bfloat16))
    results = lax.map(one_group, (grouped_queries, key_groups, value_groups, gradient_groups))
    attn_out = jnp.transpose(results[0], (2, 0, 1, 3)).reshape(DOCUMENT_TOKENS, QUERY_HEADS, HEAD_SIZE)
    grad_queries = jnp.transpose(results[1], (2, 0, 1, 3)).reshape(DOCUMENT_TOKENS, QUERY_HEADS, HEAD_SIZE)
    grad_keys = jnp.transpose(results[2], (1, 0, 2))
    grad_values = jnp.transpose(results[3], (1, 0, 2))
    return (attn_out, grad_queries, grad_keys, grad_values)
```

```python
import functools
import math

import jax
import jax.numpy as jnp
from jax import lax
from jax.experimental import pallas as pl
from jax.experimental.pallas import tpu as pltpu
from jax.sharding import PartitionSpec as P

NEG_FILL = -1e30
TILE = 256
BLOCK = 64


def dot_nt(a, b):
    return lax.dot_general(a, b, (((1,), (1,)), ((), ())), preferred_element_type=jnp.float32)


def dot_nn(a, b):
    return lax.dot_general(a, b, (((1,), (0,)), ((), ())), preferred_element_type=jnp.float32)


def forward_kernel(
    order_ref, place_ref, q_own, q_far, g_own, g_far, kv_ref, p_ref, o_ref, stat_ref, vt_ref,
    *, own_tiles, repeat, scale
):
    step = pl.program_id(0)
    holders, _, rows, width = kv_ref.shape
    chunks = holders * rows // TILE
    per = TILE // rows

    @pl.when(step == 0)
    def _():
        for c in range(chunks):
            vals = kv_ref[c * per : (c + 1) * per, 1].reshape(TILE, width)
            vt_ref[:, c * TILE : (c + 1) * TILE] = vals.astype(jnp.float32).T.astype(jnp.bfloat16)

    mine = step < own_tiles
    q = jnp.where(mine, q_own[...], q_far[...])
    g = jnp.where(mine, g_own[...], g_far[...])
    side = place_ref[0] % 2
    ctx = jnp.where(mine, place_ref[0], place_ref[0] + 1 - 2 * side)
    token = lax.rem(step, own_tiles) * (TILE // repeat)
    blocks_here = rows // BLOCK
    row_place = order_ref[ctx * blocks_here + token // BLOCK] * BLOCK + token % BLOCK
    diff = lax.broadcasted_iota(jnp.int32, (BLOCK, TILE), 0) - (
        lax.broadcasted_iota(jnp.int32, (BLOCK, TILE), 1) // repeat
    )
    scaled = []
    top = None
    for c in range(chunks):
        keys = kv_ref[c * per : (c + 1) * per, 0].reshape(TILE, width)
        s = dot_nt(keys, q) * scale
        parts = []
        for b in range(TILE // BLOCK):
            at = c * (TILE // BLOCK) + b
            stored = ((at // blocks_here) * 2 + side) * blocks_here + at % blocks_here
            limit = row_place - order_ref[stored] * BLOCK
            parts.append(jnp.where(diff <= limit, s[b * BLOCK : (b + 1) * BLOCK], NEG_FILL))
        s = jnp.concatenate(parts, axis=0)
        scaled.append(s)
        here = jnp.max(s, axis=0, keepdims=True)
        top = here if top is None else jnp.maximum(top, here)
    total = jnp.zeros((1, TILE), jnp.float32)
    out = jnp.zeros((width, TILE), jnp.float32)
    for c in range(chunks):
        p = jnp.exp2(scaled[c] - top)
        total = total + jnp.sum(p, axis=0, keepdims=True)
        p = p.astype(jnp.bfloat16)
        p_ref[0, c * TILE : (c + 1) * TILE] = p
        out = out + dot_nn(vt_ref[:, c * TILE : (c + 1) * TILE], p)
    o_ref[0] = out
    delta = jnp.sum(out * g.astype(jnp.float32).T, axis=0, keepdims=True)
    stat_ref[0, 0:1] = top
    stat_ref[0, 1:2] = total
    stat_ref[0, 2:3] = delta
    stat_ref[0, 3:8] = jnp.zeros((5, TILE), jnp.float32)


def backward_kernel(
    q_own, q_far, g_own, g_far, kv_ref, p_ref, o_ref, here_ref, there_ref,
    dkv_ref, o_own, dq_own, send_ref, kt_ref, dk_ref, dv_ref,
    *, own_tiles, scale
):
    step = pl.program_id(0)
    holders, _, rows, width = kv_ref.shape
    chunks = holders * rows // TILE
    per = TILE // rows

    @pl.when(step == 0)
    def _():
        for c in range(chunks):
            keys = kv_ref[c * per : (c + 1) * per, 0].reshape(TILE, width)
            kt_ref[:, c * TILE : (c + 1) * TILE] = keys.astype(jnp.float32).T.astype(jnp.bfloat16)
        dk_ref[...] = jnp.zeros_like(dk_ref)
        dv_ref[...] = jnp.zeros_like(dv_ref)

    mine = step < own_tiles
    q = jnp.where(mine, q_own[...], q_far[...])
    g = jnp.where(mine, g_own[...], g_far[...])
    top_a, sum_a, delta_a = here_ref[0, 0:1], here_ref[0, 1:2], here_ref[0, 2:3]
    top_b, sum_b, delta_b = there_ref[0, 0:1], there_ref[0, 1:2], there_ref[0, 2:3]
    top = jnp.maximum(top_a, top_b)
    fa, fb = jnp.exp2(top_a - top), jnp.exp2(top_b - top)
    inverse = 1.0 / (sum_a * fa + sum_b * fb)
    factor = fa * inverse
    delta = (delta_a * fa + delta_b * fb) * inverse
    dq = jnp.zeros((width, TILE), jnp.float32)
    for c in range(chunks):
        span = slice(c * TILE, (c + 1) * TILE)
        vals = kv_ref[c * per : (c + 1) * per, 1].reshape(TILE, width)
        probs = p_ref[0, span].astype(jnp.float32) * factor
        grad_probs = dot_nt(vals, g)
        grad = (probs * (grad_probs - delta)).astype(jnp.bfloat16)
        dv_ref[span] += dot_nn(probs.astype(jnp.bfloat16), g)
        dk_ref[span] += dot_nn(grad, q)
        dq = dq + dot_nn(kt_ref[:, span], grad)
    dq = (dq * scale).T
    o = (o_ref[0] * factor).T

    @pl.when(mine)
    def _():
        o_own[...] = o
        dq_own[...] = dq

    @pl.when(jnp.logical_not(mine))
    def _():
        send_ref[0] = o.astype(jnp.bfloat16)
        send_ref[1] = dq.astype(jnp.bfloat16)

    @pl.when(step == pl.num_programs(0) - 1)
    def _():
        for z in range(holders):
            dkv_ref[z, 0] = (dk_ref[z * rows : (z + 1) * rows] * scale).astype(jnp.bfloat16)
            dkv_ref[z, 1] = dv_ref[z * rows : (z + 1) * rows].astype(jnp.bfloat16)


def shards(queries, keys, values, output_gradient, block_order):
    tok, heads, width = queries.shape
    ctx_size = lax.axis_size("ctx")
    holders = ctx_size // 2
    columns = [[2 * z + x for z in range(holders)] for x in range(2)]
    swap = [(i, i ^ 1) for i in range(ctx_size)]
    own_rows = tok * heads
    own_tiles = own_rows // TILE
    tiles = 2 * own_tiles
    col_keys = holders * tok
    score_scale = 1.0 / math.sqrt(width)

    q = queries.reshape(own_rows, width)
    g = output_gradient.reshape(own_rows, width)
    kv = jnp.stack([keys.reshape(tok, width), values.reshape(tok, width)])
    spread = jnp.broadcast_to(kv[None], (holders, 2, tok, width))
    kv_all = lax.all_to_all(spread, "ctx", 0, 0, axis_index_groups=columns, tiled=True)
    q_far = lax.ppermute(q, "ctx", swap)
    g_far = lax.ppermute(g, "ctx", swap)
    place = lax.axis_index("ctx").astype(jnp.int32).reshape(1)

    own_map = lambda i: (jnp.minimum(i, own_tiles - 1), 0)
    far_map = lambda i: (jnp.maximum(i - own_tiles, 0), 0)
    row_specs = [
        pl.BlockSpec((TILE, width), own_map),
        pl.BlockSpec((TILE, width), far_map),
        pl.BlockSpec((TILE, width), own_map),
        pl.BlockSpec((TILE, width), far_map),
        pl.BlockSpec((holders, 2, tok, width), lambda i: (0, 0, 0, 0)),
    ]
    smem = pl.BlockSpec(memory_space=pltpu.SMEM)
    p_spec = pl.BlockSpec((1, col_keys, TILE), lambda i: (i, 0, 0))
    o_spec = pl.BlockSpec((1, width, TILE), lambda i: (i, 0, 0))
    stat_spec = pl.BlockSpec((1, 8, TILE), lambda i: (i, 0, 0))
    pairs = 2 * own_rows * col_keys
    weights, partial_out, stats = pl.pallas_call(
        functools.partial(
            forward_kernel, own_tiles=own_tiles, repeat=heads,
            scale=score_scale * math.log2(math.e),
        ),
        grid=(tiles,),
        in_specs=[smem, smem] + row_specs,
        out_specs=[p_spec, o_spec, stat_spec],
        out_shape=[
            jax.ShapeDtypeStruct((tiles, col_keys, TILE), jnp.bfloat16),
            jax.ShapeDtypeStruct((tiles, width, TILE), jnp.float32),
            jax.ShapeDtypeStruct((tiles, 8, TILE), jnp.float32),
        ],
        scratch_shapes=[pltpu.VMEM((width, col_keys), jnp.bfloat16)],
        compiler_params=pltpu.CompilerParams(vmem_limit_bytes=40 * 2**20),
        cost_estimate=pl.CostEstimate(
            flops=4 * pairs * width, bytes_accessed=2 * pairs, transcendentals=pairs
        ),
        name="forward",
    )(block_order, place, q, q_far, g, g_far, kv_all)

    far_stats = lax.ppermute(stats, "ctx", swap)

    dkv, o_own, dq_own, send = pl.pallas_call(
        functools.partial(backward_kernel, own_tiles=own_tiles, scale=score_scale),
        grid=(tiles,),
        in_specs=row_specs
        + [
            p_spec,
            o_spec,
            stat_spec,
            pl.BlockSpec((1, 8, TILE), lambda i: (lax.rem(i + own_tiles, tiles), 0, 0)),
        ],
        out_specs=[
            pl.BlockSpec((holders, 2, tok, width), lambda i: (0, 0, 0, 0)),
            pl.BlockSpec((TILE, width), own_map),
            pl.BlockSpec((TILE, width), own_map),
            pl.BlockSpec((2, TILE, width), lambda i: (0, jnp.maximum(i - own_tiles, 0), 0)),
        ],
        out_shape=[
            jax.ShapeDtypeStruct((holders, 2, tok, width), jnp.bfloat16),
            jax.ShapeDtypeStruct((own_rows, width), jnp.float32),
            jax.ShapeDtypeStruct((own_rows, width), jnp.float32),
            jax.ShapeDtypeStruct((2, own_rows, width), jnp.bfloat16),
        ],
        scratch_shapes=[
            pltpu.VMEM((width, col_keys), jnp.bfloat16),
            pltpu.VMEM((col_keys, width), jnp.float32),
            pltpu.VMEM((col_keys, width), jnp.float32),
        ],
        compiler_params=pltpu.CompilerParams(vmem_limit_bytes=40 * 2**20),
        cost_estimate=pl.CostEstimate(
            flops=8 * pairs * width, bytes_accessed=2 * pairs, transcendentals=0
        ),
        name="backward",
    )(q, q_far, g, g_far, kv_all, weights, partial_out, stats, far_stats)

    terms = lax.all_to_all(dkv, "ctx", 0, 0, axis_index_groups=columns, tiled=True)
    received = lax.ppermute(send, "ctx", swap).astype(jnp.float32)
    attn_out = (o_own + received[0]).astype(jnp.bfloat16).reshape(tok, heads, width)
    grad_queries = (dq_own + received[1]).astype(jnp.bfloat16).reshape(tok, heads, width)
    summed = jnp.sum(terms.astype(jnp.float32), axis=0).astype(jnp.bfloat16)
    grad_keys = summed[0].reshape(tok, 1, width)
    grad_values = summed[1].reshape(tok, 1, width)
    return attn_out, grad_queries, grad_keys, grad_values


def solution(mesh):
    tokens = P(("dp", "ctx"), "head", None)
    return jax.shard_map(
        shards,
        mesh=mesh,
        in_specs=(tokens, tokens, tokens, tokens, P("dp")),
        out_specs=(tokens, tokens, tokens, tokens),
        check_vma=False,
    )
```

```python
import functools
import math

import jax
import jax.numpy as jnp
from jax import lax
from jax.experimental import pallas as pl
from jax.experimental.pallas import tpu as pltpu
from jax.sharding import PartitionSpec as P

NEG_FILL = -1e30
TILE = 256
BLOCK = 64
VMEM = pl.BlockSpec(memory_space=pltpu.VMEM)
SMEM = pl.BlockSpec(memory_space=pltpu.SMEM)
HBM = pl.BlockSpec(memory_space=pltpu.HBM)
F32 = jnp.float32
HALF = jnp.bfloat16


def dot_nt(a, b):
    return lax.dot_general(a, b, (((1,), (1,)), ((), ())), preferred_element_type=F32)


def dot_nn(a, b):
    return lax.dot_general(a, b, (((1,), (0,)), ((), ())), preferred_element_type=F32)


def flipped(a):
    return a.astype(F32).T


def spread_kernel(k_ref, v_ref, out_ref, held, sems):
    loads = [
        pltpu.make_async_copy(ref, held.at[i], sems.at[i]) for i, ref in enumerate((k_ref, v_ref))
    ]
    for load in loads:
        load.start()
    for load in loads:
        load.wait()
    stores = [
        pltpu.make_async_copy(held, out_ref.at[z], sems.at[2 + z]) for z in range(out_ref.shape[0])
    ]
    for store in stores:
        store.start()
    for store in stores:
        store.wait()


def stage_kernel(q_ref, g_ref, q_out, g_out, gt_out):
    q_out[...] = q_ref[...]
    g_out[...] = g_ref[...]
    for t in range(gt_out.shape[0]):
        gt_out[t] = flipped(g_ref[t * TILE : (t + 1) * TILE]).astype(HALF)


def flip_kernel(g_ref, gt_out):
    for t in range(gt_out.shape[0]):
        gt_out[t] = flipped(g_ref[t * TILE : (t + 1) * TILE]).astype(HALF)


def forward_kernel(
    info_ref, q_own, q_far, gt_own, gt_far, kv_ref, p_ref, o_own, o_far, stat_ref, vt_ref, s_ref,
    *, repeat, scale
):
    holders, _, rows, width = kv_ref.shape
    col_keys = holders * rows
    chunks = col_keys // TILE
    per = TILE // rows
    own_tiles = o_own.shape[0]
    blocks_here = rows // BLOCK
    ctx = info_ref[info_ref.shape[0] - 1]
    side = ctx % 2

    for c in range(chunks):
        vals = kv_ref[c * per : (c + 1) * per, 1].reshape(TILE, width)
        vt_ref[:width, c * TILE : (c + 1) * TILE] = flipped(vals).astype(HALF)
    vt_ref[width:] = jnp.ones((vt_ref.shape[0] - width, col_keys), HALF)
    diff = lax.broadcasted_iota(jnp.int32, (BLOCK, TILE), 0) - (
        lax.broadcasted_iota(jnp.int32, (BLOCK, TILE), 1) // repeat
    )

    def scores(tile):
        mine = tile < own_tiles
        device = ctx if mine else ctx + 1 - 2 * side
        local = tile % own_tiles
        token = local * (TILE // repeat)
        place = info_ref[device * blocks_here + token // BLOCK] * BLOCK + token % BLOCK
        q = (q_own if mine else q_far)[local * TILE : (local + 1) * TILE]
        top = None
        for c in range(chunks):
            keys = kv_ref[c * per : (c + 1) * per, 0].reshape(TILE, width)
            s = dot_nt(keys, q) * scale
            parts = []
            for b in range(TILE // BLOCK):
                at = c * (TILE // BLOCK) + b
                stored = ((at // blocks_here) * 2 + side) * blocks_here + at % blocks_here
                limit = place - info_ref[stored] * BLOCK
                parts.append(jnp.where(diff <= limit, s[b * BLOCK : (b + 1) * BLOCK], NEG_FILL))
            s = jnp.concatenate(parts, axis=0)
            s_ref[tile % 2, c * TILE : (c + 1) * TILE] = s
            here = jnp.max(s.reshape(TILE // 8, 8, TILE), axis=0)
            top = here if top is None else jnp.maximum(top, here)
        return jnp.max(top, axis=0, keepdims=True)

    def weigh(tile, top):
        out = None
        for c in range(chunks):
            span = slice(c * TILE, (c + 1) * TILE)
            p = jnp.exp2(s_ref[tile % 2, span] - top).astype(HALF)
            p_ref[span, tile * TILE : (tile + 1) * TILE] = p
            o = dot_nn(vt_ref[:, span], p)
            out = o if out is None else out + o
        total, out = out[width : width + 1], out[:width]
        mine = tile < own_tiles
        local = tile % own_tiles
        if mine:
            o_own[local] = out
        else:
            o_far[local] = out.astype(HALF)
        stat_ref[tile, 0:1] = top
        stat_ref[tile, 1:2] = total
        stat_ref[tile, 2:3] = jnp.sum(
            out * (gt_own if mine else gt_far)[local].astype(F32), axis=0, keepdims=True
        )
        stat_ref[tile, 3:8] = jnp.zeros((5, TILE), F32)

    top = scores(0)
    for tile in range(2 * own_tiles):
        later = scores(tile + 1) if tile + 1 < 2 * own_tiles else None
        weigh(tile, top)
        top = later


def backward_kernel(
    q_own, q_far, g_own, g_far, gt_own, gt_far, kv_ref, p_ref, here_ref, there_ref,
    dkv_ref, dq_own, dq_far, factor_ref, qs_ref, gs_ref, ds_ref, kt_ref, done_ref, sems,
    *, scale
):
    holders, _, rows, width = kv_ref.shape
    chunks = holders * rows // TILE
    per = TILE // rows
    own_tiles = gt_own.shape[0]
    tiles = 2 * own_tiles
    flip_keys(kv_ref, kt_ref)
    deltas, factors = [], []
    for tile in range(tiles):
        mine = tile < own_tiles
        local = tile % own_tiles
        other = (tile + own_tiles) % tiles
        top_a, sum_a, delta_a = (here_ref[tile, i : i + 1] for i in range(3))
        top_b, sum_b, delta_b = (there_ref[other, i : i + 1] for i in range(3))
        top = jnp.maximum(top_a, top_b)
        fa, fb = jnp.exp2(top_a - top), jnp.exp2(top_b - top)
        inverse = 1.0 / (sum_a * fa + sum_b * fb)
        factor = fa * inverse
        deltas.append((delta_a * fa + delta_b * fb) * inverse)
        factors.append(factor)
        if mine:
            factor_ref[tile, 0:1] = factor
            factor_ref[tile, 1:2] = fb * inverse
            factor_ref[tile, 2:8] = jnp.zeros((6, TILE), F32)
        down = jnp.broadcast_to(factor, (8, TILE)).T[:, 0:1]
        span = slice(local * TILE, (local + 1) * TILE)
        put = slice(tile * TILE, (tile + 1) * TILE)
        qs_ref[put] = ((q_own if mine else q_far)[span].astype(F32) * down).astype(HALF)
        gs_ref[put] = ((g_own if mine else g_far)[span].astype(F32) * down).astype(HALF)

    def grads(c):
        span = slice(c * TILE, (c + 1) * TILE)
        vals = kv_ref[c * per : (c + 1) * per, 1].reshape(TILE, width)
        for tile in range(tiles):
            mine = tile < own_tiles
            local = tile % own_tiles
            p = p_ref[span, tile * TILE : (tile + 1) * TILE].astype(F32)
            grad = p * (dot_nn(vals, (gt_own if mine else gt_far)[local]) - deltas[tile])
            ds_ref[span, tile * TILE : (tile + 1) * TILE] = grad.astype(HALF)

    copies = []
    grads(0)
    for c in range(chunks):
        span = slice(c * TILE, (c + 1) * TILE)
        if c + 1 < chunks:
            grads(c + 1)
        dv = dot_nn(p_ref[span], gs_ref[...])
        dk = dot_nn(ds_ref[span], qs_ref[...])
        for z in range(per):
            at = c * per + z
            done_ref[at, 0] = (dk[z * rows : (z + 1) * rows] * scale).astype(HALF)
            done_ref[at, 1] = dv[z * rows : (z + 1) * rows].astype(HALF)
            copies.append(pltpu.make_async_copy(done_ref.at[at], dkv_ref.at[at], sems.at[at]))
            copies[-1].start()
    for tile in range(tiles):
        dq = dot_nn(kt_ref[...], ds_ref[:, tile * TILE : (tile + 1) * TILE])
        dq = dq * (factors[tile] * scale)
        if tile < own_tiles:
            dq_own[tile] = dq
        else:
            dq_far[tile - own_tiles] = dq.astype(HALF)
    for copy in copies:
        copy.wait()


def flip_keys(kv_ref, kt_ref):
    holders, _, rows, width = kv_ref.shape
    per = TILE // rows
    for c in range(holders // per):
        keys = kv_ref[c * per : (c + 1) * per, 0].reshape(TILE, width)
        kt_ref[:, c * TILE : (c + 1) * TILE] = flipped(keys).astype(HALF)


def out_kernel(factor_ref, o_own, o_recv, out_ref):
    for t in range(o_own.shape[0]):
        o = o_own[t] * factor_ref[t, 0:1] + o_recv[t].astype(F32) * factor_ref[t, 1:2]
        out_ref[t * TILE : (t + 1) * TILE] = o.T.astype(HALF)


def join_kernel(dq_own, dq_recv, out_ref):
    for t in range(dq_own.shape[0]):
        dq = dq_own[t] + dq_recv[t].astype(F32)
        out_ref[t * TILE : (t + 1) * TILE] = dq.T.astype(HALF)


def total_kernel(terms_ref, dk_ref, dv_ref):
    for i, out in enumerate((dk_ref, dv_ref)):
        total = terms_ref[0, i].astype(F32)
        for z in range(1, terms_ref.shape[0]):
            total = total + terms_ref[z, i].astype(F32)
        out[...] = total.astype(HALF)


def call(kernel, name, ins, outs, scratch=(), flops=0, moved=0, exps=0, specs=None, out_specs=None, limit=24):
    return pl.pallas_call(
        kernel,
        in_specs=specs or [VMEM] * len(ins),
        out_specs=out_specs or [VMEM] * len(outs),
        out_shape=[jax.ShapeDtypeStruct(s, d) for s, d in outs],
        scratch_shapes=scratch,
        compiler_params=pltpu.CompilerParams(vmem_limit_bytes=limit * 2**20),
        cost_estimate=pl.CostEstimate(flops=flops, bytes_accessed=moved, transcendentals=exps),
        name=name,
    )(*ins)


def shards(queries, keys, values, output_gradient, block_order):
    tok, heads, width = queries.shape
    ctx_size = lax.axis_size("ctx")
    holders = ctx_size // 2
    columns = [[2 * z + x for z in range(holders)] for x in range(2)]
    swap = [(i, i ^ 1) for i in range(ctx_size)]
    own_rows = tok * heads
    own_tiles = own_rows // TILE
    tiles = 2 * own_tiles
    col_keys = holders * tok
    score_scale = 1.0 / math.sqrt(width)
    product = 2 * own_rows * col_keys * width
    flip_shape = (own_tiles, width, TILE)
    kv_shape = (holders, 2, tok, width)
    flat_shape = (own_rows, width)
    moved = own_rows * width * 8

    q = queries.reshape(flat_shape)
    g = output_gradient.reshape(flat_shape)
    (spread,) = call(
        spread_kernel, "spread", (keys.reshape(tok, width), values.reshape(tok, width)),
        [(kv_shape, HALF)], [pltpu.VMEM((2, tok, width), HALF), pltpu.SemaphoreType.DMA((2 + holders,))],
        moved=2 * col_keys * width, specs=[HBM, HBM], out_specs=[HBM], limit=60,
    )
    kv_all = lax.all_to_all(spread, "ctx", 0, 0, axis_index_groups=columns, tiled=True)
    q_far = lax.ppermute(q, "ctx", swap)
    g_far = lax.ppermute(g, "ctx", swap)
    info = jnp.concatenate([block_order, lax.axis_index("ctx").astype(jnp.int32).reshape(1)])
    q, g, gt_own = call(
        stage_kernel, "stage", (q, g), [(flat_shape, HALF), (flat_shape, HALF), (flip_shape, HALF)],
        moved=moved,
    )
    (gt_far,) = call(flip_kernel, "flip", (g_far,), [(flip_shape, HALF)], moved=moved)

    weights, o_own, o_far, stats = call(
        functools.partial(
            forward_kernel, repeat=heads, scale=score_scale * math.log2(math.e)
        ),
        "forward", (info, q, q_far, gt_own, gt_far, kv_all),
        [
            ((col_keys, 2 * own_rows), HALF),
            (flip_shape, F32),
            (flip_shape, HALF),
            ((tiles, 8, TILE), F32),
        ],
        [pltpu.VMEM((width + 16, col_keys), HALF), pltpu.VMEM((2, col_keys, TILE), F32)],
        flops=4 * product, exps=2 * own_rows * col_keys, specs=[SMEM] + [VMEM] * 5,
    )
    far_stats = lax.ppermute(stats, "ctx", swap)
    o_recv = lax.ppermute(o_far, "ctx", swap)

    dkv, dq_own, dq_far, factors = call(
        functools.partial(backward_kernel, scale=score_scale),
        "backward",
        (q, q_far, g, g_far, gt_own, gt_far, kv_all, weights, stats, far_stats),
        [
            (kv_shape, HALF),
            (flip_shape, F32),
            (flip_shape, HALF),
            ((own_tiles, 8, TILE), F32),
        ],
        [
            pltpu.VMEM((2 * own_rows, width), HALF),
            pltpu.VMEM((2 * own_rows, width), HALF),
            pltpu.VMEM((col_keys, 2 * own_rows), HALF),
            pltpu.VMEM((width, col_keys), HALF),
            pltpu.VMEM(kv_shape, HALF),
            pltpu.SemaphoreType.DMA((holders,)),
        ],
        flops=8 * product, out_specs=[HBM, VMEM, VMEM, VMEM],
    )
    terms = lax.all_to_all(dkv, "ctx", 0, 0, axis_index_groups=columns, tiled=True)

    dq_recv = lax.ppermute(dq_far, "ctx", swap)
    (attn_out,) = call(
        out_kernel, "out", (factors, o_own, o_recv), [(flat_shape, HALF)], moved=moved
    )
    (grad_queries,) = call(
        join_kernel, "join", (dq_own, dq_recv), [(flat_shape, HALF)], moved=moved
    )
    grad_keys, grad_values = call(
        total_kernel, "total", (terms,), [((tok, width), HALF), ((tok, width), HALF)],
        moved=2 * col_keys * width * 2,
    )
    return (
        attn_out.reshape(tok, heads, width),
        grad_queries.reshape(tok, heads, width),
        grad_keys.reshape(tok, 1, width),
        grad_values.reshape(tok, 1, width),
    )


def solution(mesh):
    tokens = P(("dp", "ctx"), "head", None)
    return jax.shard_map(
        shards,
        mesh=mesh,
        in_specs=(tokens, tokens, tokens, tokens, P("dp")),
        out_specs=(tokens, tokens, tokens, tokens),
        check_vma=False,
    )
```

```python
import functools
import math

import jax
import jax.numpy as jnp
from jax import lax
from jax.experimental import pallas as pl
from jax.experimental.pallas import tpu as pltpu
from jax.sharding import PartitionSpec as P

NEG_FILL = -1e30
TILE = 256
BLOCK = 64
VMEM = pl.BlockSpec(memory_space=pltpu.VMEM)
SMEM = pl.BlockSpec(memory_space=pltpu.SMEM)
HBM = pl.BlockSpec(memory_space=pltpu.HBM)
F32 = jnp.float32
HALF = jnp.bfloat16


def dot_nt(a, b):
    return lax.dot_general(a, b, (((1,), (1,)), ((), ())), preferred_element_type=F32)


def dot_nn(a, b):
    return lax.dot_general(a, b, (((1,), (0,)), ((), ())), preferred_element_type=F32)


def flipped(a):
    return a.astype(F32).T


def spread_kernel(k_ref, v_ref, out_ref, held, sems):
    loads = [
        pltpu.make_async_copy(ref, held.at[i], sems.at[i]) for i, ref in enumerate((k_ref, v_ref))
    ]
    for load in loads:
        load.start()
    for load in loads:
        load.wait()
    stores = [
        pltpu.make_async_copy(held, out_ref.at[z], sems.at[2 + z]) for z in range(out_ref.shape[0])
    ]
    for store in stores:
        store.start()
    for store in stores:
        store.wait()


def flip_rows(source, out_ref):
    for t in range(out_ref.shape[0]):
        out_ref[t] = flipped(source[t * TILE : (t + 1) * TILE]).astype(HALF)


def stage_kernel(info_ref, q_ref, g_ref, qt_out, gt_out, limit_ref, side_ref, *, repeat):
    own_tiles = gt_out.shape[0]
    tiles, blocks, _ = limit_ref.shape
    last = info_ref.shape[0] - 1
    ctx = info_ref[last]
    side = ctx % 2
    blocks_here = own_tiles * TILE // repeat // BLOCK
    flip_rows(q_ref, qt_out)
    flip_rows(g_ref, gt_out)
    token_of = lax.broadcasted_iota(jnp.int32, (1, TILE), 1) // repeat
    for t in range(tiles):
        device = ctx if t < own_tiles else ctx + 1 - 2 * side
        token = (t % own_tiles) * (TILE // repeat)
        place = info_ref[device * blocks_here + token // BLOCK] * BLOCK + token % BLOCK
        for b in range(blocks):
            stored = ((b // blocks_here) * 2 + side) * blocks_here + b % blocks_here
            limit_ref[t, b : b + 1] = token_of + (place - info_ref[stored] * BLOCK)
    side_ref[...] = jnp.zeros(side_ref.shape, jnp.int32) + side


def flip_kernel(q_ref, g_ref, qt_out, gt_out):
    flip_rows(q_ref, qt_out)
    flip_rows(g_ref, gt_out)


def forward_kernel(
    limit_ref, qt_own, qt_far, gt_own, gt_far, kv_ref, p_ref, o_own, o_far, stat_ref, vt_ref, s_ref,
    *, scale
):
    holders, _, rows, width = kv_ref.shape
    col_keys = holders * rows
    chunks = col_keys // TILE
    per = TILE // rows
    own_tiles = o_own.shape[0]

    for c in range(chunks):
        vals = kv_ref[c * per : (c + 1) * per, 1].reshape(TILE, width)
        vt_ref[:width, c * TILE : (c + 1) * TILE] = flipped(vals).astype(HALF)
    vt_ref[width:] = jnp.ones((vt_ref.shape[0] - width, col_keys), HALF)
    key_of = lax.broadcasted_iota(jnp.int32, (BLOCK, TILE), 0)

    def scores(tile):
        mine = tile < own_tiles
        local = tile % own_tiles
        qt = (qt_own if mine else qt_far)[local]
        top = None
        for c in range(chunks):
            keys = kv_ref[c * per : (c + 1) * per, 0].reshape(TILE, width)
            s = dot_nn(keys, qt) * scale
            parts = []
            for b in range(TILE // BLOCK):
                at = c * (TILE // BLOCK) + b
                seen = key_of <= limit_ref[tile, at : at + 1]
                parts.append(jnp.where(seen, s[b * BLOCK : (b + 1) * BLOCK], NEG_FILL))
            s = jnp.concatenate(parts, axis=0)
            s_ref[tile % 2, c * TILE : (c + 1) * TILE] = s
            here = jnp.max(s.reshape(TILE // 8, 8, TILE), axis=0)
            top = here if top is None else jnp.maximum(top, here)
        return jnp.max(top, axis=0, keepdims=True)

    def weigh(tile, top):
        put = slice(tile * TILE, (tile + 1) * TILE)
        for c in range(chunks):
            span = slice(c * TILE, (c + 1) * TILE)
            p_ref[span, put] = jnp.exp2(s_ref[tile % 2, span] - top).astype(HALF)
        out = dot_nn(vt_ref[...], p_ref[:, put])
        total, out = out[width : width + 1], out[:width]
        mine = tile < own_tiles
        local = tile % own_tiles
        if mine:
            o_own[local] = out
        else:
            o_far[local] = out.astype(HALF)
        delta = jnp.sum(
            out * (gt_own if mine else gt_far)[local].astype(F32), axis=0, keepdims=True
        )
        stat_ref[3 * tile : 3 * tile + 3] = jnp.concatenate([top, total, delta], axis=0)

    top = scores(0)
    for tile in range(2 * own_tiles):
        later = scores(tile + 1) if tile + 1 < 2 * own_tiles else None
        weigh(tile, top)
        top = later


def backward_kernel(
    side_ref, qt_own, qt_far, gt_own, gt_far, kv_ref, p_ref, stat_ref,
    dkv_ref, dq_own, dq_far, factor_ref, qs_ref, gs_ref, ds_ref, kt_ref, done_ref, sems,
    *, scale
):
    holders, _, rows, width = kv_ref.shape
    chunks = holders * rows // TILE
    per = TILE // rows
    own_tiles = gt_own.shape[0]
    tiles = 2 * own_tiles
    flip_keys(kv_ref, kt_ref)
    deltas, factors = [], []
    right = side_ref[0:1] > 0
    for tile in range(tiles):
        mine = tile < own_tiles
        local = tile % own_tiles
        other = (tile + own_tiles) % tiles
        here, there = (
            [jnp.where(right, stat_ref[1 - s, at], stat_ref[s, at]) for at in spans]
            for s, spans in (
                (0, [slice(3 * tile + i, 3 * tile + i + 1) for i in range(3)]),
                (1, [slice(3 * other + i, 3 * other + i + 1) for i in range(3)]),
            )
        )
        top_a, sum_a, delta_a = here
        top_b, sum_b, delta_b = there
        top = jnp.maximum(top_a, top_b)
        fa, fb = jnp.exp2(top_a - top), jnp.exp2(top_b - top)
        inverse = 1.0 / (sum_a * fa + sum_b * fb)
        factor = fa * inverse
        deltas.append((delta_a * fa + delta_b * fb) * inverse)
        factors.append(factor)
        factor_ref[tile, 0:1] = factor
        factor_ref[tile, 1:2] = fb * inverse
        factor_ref[tile, 2:8] = jnp.zeros((6, TILE), F32)
        put = slice(tile * TILE, (tile + 1) * TILE)
        for source, target in (
            (qt_own if mine else qt_far, qs_ref),
            (gt_own if mine else gt_far, gs_ref),
        ):
            target[put] = (source[local].astype(F32) * factor).T.astype(HALF)

    def grads(c):
        span = slice(c * TILE, (c + 1) * TILE)
        vals = kv_ref[c * per : (c + 1) * per, 1].reshape(TILE, width)
        for tile in range(tiles):
            mine = tile < own_tiles
            local = tile % own_tiles
            p = p_ref[span, tile * TILE : (tile + 1) * TILE].astype(F32)
            grad = p * (dot_nn(vals, (gt_own if mine else gt_far)[local]) - deltas[tile])
            ds_ref[span, tile * TILE : (tile + 1) * TILE] = grad.astype(HALF)

    copies = []
    grads(0)
    for c in range(chunks):
        span = slice(c * TILE, (c + 1) * TILE)
        if c + 1 < chunks:
            grads(c + 1)
        dv = dot_nn(p_ref[span], gs_ref[...])
        dk = dot_nn(ds_ref[span], qs_ref[...])
        for z in range(per):
            at = c * per + z
            done_ref[at, 0] = (dk[z * rows : (z + 1) * rows] * scale).astype(HALF)
            done_ref[at, 1] = dv[z * rows : (z + 1) * rows].astype(HALF)
            copies.append(pltpu.make_async_copy(done_ref.at[at], dkv_ref.at[at], sems.at[at]))
            copies[-1].start()
    for tile in range(tiles):
        dq = dot_nn(kt_ref[...], ds_ref[:, tile * TILE : (tile + 1) * TILE])
        dq = (dq * (factors[tile] * scale)).astype(HALF)
        (dq_own if tile < own_tiles else dq_far)[tile % own_tiles] = dq
    for copy in copies:
        copy.wait()


def flip_keys(kv_ref, kt_ref):
    holders, _, rows, width = kv_ref.shape
    per = TILE // rows
    for c in range(holders // per):
        keys = kv_ref[c * per : (c + 1) * per, 0].reshape(TILE, width)
        kt_ref[:, c * TILE : (c + 1) * TILE] = flipped(keys).astype(HALF)


def out_kernel(factor_ref, o_own, o_recv, out_ref):
    for t in range(o_own.shape[0]):
        o = o_own[t] * factor_ref[t, 0:1] + o_recv[t].astype(F32) * factor_ref[t, 1:2]
        out_ref[t * TILE : (t + 1) * TILE] = o.T.astype(HALF)


def pack_kernel(dq_ref, out_ref):
    out_ref[...] = dq_ref[...]


def join_kernel(dq_own, dq_recv, out_ref):
    for t in range(dq_own.shape[0]):
        dq = dq_own[t].astype(F32) + dq_recv[t].astype(F32)
        out_ref[t * TILE : (t + 1) * TILE] = dq.T.astype(HALF)


def total_kernel(terms_ref, dk_ref, dv_ref):
    for i, out in enumerate((dk_ref, dv_ref)):
        total = terms_ref[0, i].astype(F32)
        for z in range(1, terms_ref.shape[0]):
            total = total + terms_ref[z, i].astype(F32)
        out[...] = total.astype(HALF)


def call(kernel, name, ins, outs, scratch=(), flops=0, moved=0, exps=0, specs=None, out_specs=None, limit=8):
    return pl.pallas_call(
        kernel,
        in_specs=specs or [VMEM] * len(ins),
        out_specs=out_specs or [VMEM] * len(outs),
        out_shape=[jax.ShapeDtypeStruct(s, d) for s, d in outs],
        scratch_shapes=scratch,
        compiler_params=pltpu.CompilerParams(vmem_limit_bytes=limit * 2**20),
        cost_estimate=pl.CostEstimate(flops=flops, bytes_accessed=moved, transcendentals=exps),
        name=name,
    )(*ins)


def shards(queries, keys, values, output_gradient, block_order):
    tok, heads, width = queries.shape
    ctx_size = lax.axis_size("ctx")
    holders = ctx_size // 2
    columns = [[2 * z + x for z in range(holders)] for x in range(2)]
    swap = [(i, i ^ 1) for i in range(ctx_size)]
    own_rows = tok * heads
    own_tiles = own_rows // TILE
    tiles = 2 * own_tiles
    col_keys = holders * tok
    score_scale = 1.0 / math.sqrt(width)
    product = 2 * own_rows * col_keys * width
    flip_shape = (own_tiles, width, TILE)
    kv_shape = (holders, 2, tok, width)
    flat_shape = (own_rows, width)
    moved = own_rows * width * 8

    q = queries.reshape(flat_shape)
    g = output_gradient.reshape(flat_shape)
    (spread,) = call(
        spread_kernel, "spread", (keys.reshape(tok, width), values.reshape(tok, width)),
        [(kv_shape, HALF)], [pltpu.VMEM((2, tok, width), HALF), pltpu.SemaphoreType.DMA((2 + holders,))],
        moved=2 * col_keys * width, specs=[HBM, HBM], out_specs=[HBM], limit=60,
    )
    kv_all = lax.all_to_all(spread, "ctx", 0, 0, axis_index_groups=columns, tiled=True)
    q_far = lax.ppermute(q, "ctx", swap)
    g_far = lax.ppermute(g, "ctx", swap)
    info = jnp.concatenate([block_order, lax.axis_index("ctx").astype(jnp.int32).reshape(1)])
    pairs = [[2 * z, 2 * z + 1] for z in range(holders)]
    qt_own, gt_own, limits, side = call(
        functools.partial(stage_kernel, repeat=heads), "stage", (info, q, g),
        [
            (flip_shape, HALF),
            (flip_shape, HALF),
            ((tiles, col_keys // BLOCK, TILE), jnp.int32),
            ((8, TILE), jnp.int32),
        ],
        moved=moved, specs=[SMEM, VMEM, VMEM],
    )
    qt_far, gt_far = call(
        flip_kernel, "flip", (q_far, g_far), [(flip_shape, HALF)] * 2, moved=moved
    )

    weights, o_own, o_far, stats = call(
        functools.partial(forward_kernel, scale=score_scale * math.log2(math.e)),
        "forward", (limits, qt_own, qt_far, gt_own, gt_far, kv_all),
        [
            ((col_keys, 2 * own_rows), HALF),
            (flip_shape, F32),
            (flip_shape, HALF),
            ((3 * tiles, TILE), F32),
        ],
        [pltpu.VMEM((width + 16, col_keys), HALF), pltpu.VMEM((2, col_keys, TILE), F32)],
        flops=4 * product, exps=2 * own_rows * col_keys, limit=12,
    )
    both = lax.all_gather(stats, "ctx", axis_index_groups=pairs)
    o_recv = lax.ppermute(o_far, "ctx", swap)

    dkv, dq_own, dq_far, factors = call(
        functools.partial(backward_kernel, scale=score_scale),
        "backward",
        (side, qt_own, qt_far, gt_own, gt_far, kv_all, weights, both),
        [
            (kv_shape, HALF),
            (flip_shape, HALF),
            (flip_shape, HALF),
            ((tiles, 8, TILE), F32),
        ],
        [
            pltpu.VMEM((2 * own_rows, width), HALF),
            pltpu.VMEM((2 * own_rows, width), HALF),
            pltpu.VMEM((col_keys, 2 * own_rows), HALF),
            pltpu.VMEM((width, col_keys), HALF),
            pltpu.VMEM(kv_shape, HALF),
            pltpu.SemaphoreType.DMA((holders,)),
        ],
        flops=8 * product, limit=16, out_specs=[HBM, VMEM, VMEM, VMEM],
    )
    terms = lax.all_to_all(dkv, "ctx", 0, 0, axis_index_groups=columns, tiled=True)

    (dq_sent,) = call(
        pack_kernel, "pack", (dq_far,), [(flip_shape, HALF)], moved=own_rows * width * 4
    )
    dq_recv = lax.ppermute(dq_sent, "ctx", swap)
    (attn_out,) = call(
        out_kernel, "out", (factors, o_own, o_recv), [(flat_shape, HALF)], moved=moved
    )
    (grad_queries,) = call(
        join_kernel, "join", (dq_own, dq_recv), [(flat_shape, HALF)], moved=moved
    )
    grad_keys, grad_values = call(
        total_kernel, "total", (terms,), [((tok, width), HALF), ((tok, width), HALF)],
        moved=2 * col_keys * width * 2,
    )
    return (
        attn_out.reshape(tok, heads, width),
        grad_queries.reshape(tok, heads, width),
        grad_keys.reshape(tok, 1, width),
        grad_values.reshape(tok, 1, width),
    )


def solution(mesh):
    tokens = P(("dp", "ctx"), "head", None)
    return jax.shard_map(
        shards,
        mesh=mesh,
        in_specs=(tokens, tokens, tokens, tokens, P("dp")),
        out_specs=(tokens, tokens, tokens, tokens),
        check_vma=False,
    )
```

```python
import functools
import math

import jax
import jax.numpy as jnp
from jax import lax
from jax.experimental import pallas as pl
from jax.experimental.pallas import tpu as pltpu
from jax.sharding import PartitionSpec as P

NEG_FILL = -1e30
WIDEST = 2.0**40
TILE = 256
BLOCK = 64
VMEM = pl.BlockSpec(memory_space=pltpu.VMEM)
SMEM = pl.BlockSpec(memory_space=pltpu.SMEM)
HBM = pl.BlockSpec(memory_space=pltpu.HBM)
F32 = jnp.float32
HALF = jnp.bfloat16


def dot_nt(a, b):
    return lax.dot_general(a, b, (((1,), (1,)), ((), ())), preferred_element_type=F32)


def dot_nn(a, b):
    return lax.dot_general(a, b, (((1,), (0,)), ((), ())), preferred_element_type=F32)


def flipped(a):
    return a.astype(F32).T


def spread_kernel(k_ref, v_ref, out_ref, held, sems):
    loads = [
        pltpu.make_async_copy(ref, held.at[i], sems.at[i]) for i, ref in enumerate((k_ref, v_ref))
    ]
    for load in loads:
        load.start()
    for load in loads:
        load.wait()
    stores = [
        pltpu.make_async_copy(held, out_ref.at[z], sems.at[2 + z]) for z in range(out_ref.shape[0])
    ]
    for store in stores:
        store.start()
    for store in stores:
        store.wait()


def flip_rows(source, out_ref):
    for t in range(out_ref.shape[0]):
        out_ref[t] = flipped(source[t * TILE : (t + 1) * TILE]).astype(HALF)


def stage_kernel(info_ref, q_ref, g_ref, qt_out, gt_out, limit_ref, side_ref, *, repeat):
    own_tiles = gt_out.shape[0]
    tiles, blocks, _ = limit_ref.shape
    last = info_ref.shape[0] - 1
    ctx = info_ref[last]
    side = ctx % 2
    blocks_here = own_tiles * TILE // repeat // BLOCK
    flip_rows(q_ref, qt_out)
    flip_rows(g_ref, gt_out)
    token_of = lax.broadcasted_iota(jnp.int32, (1, TILE), 1) // repeat
    for t in range(tiles):
        device = ctx if t < own_tiles else ctx + 1 - 2 * side
        token = (t % own_tiles) * (TILE // repeat)
        place = info_ref[device * blocks_here + token // BLOCK] * BLOCK + token % BLOCK
        for b in range(blocks):
            stored = ((b // blocks_here) * 2 + side) * blocks_here + b % blocks_here
            limit_ref[t, b : b + 1] = token_of + (place - info_ref[stored] * BLOCK)
    side_ref[...] = jnp.zeros(side_ref.shape, jnp.int32) + side


def flip_kernel(q_ref, g_ref, qt_out, gt_out):
    flip_rows(q_ref, qt_out)
    flip_rows(g_ref, gt_out)


def forward_kernel(
    limit_ref, qt_own, qt_far, gt_own, gt_far, kv_ref, p_ref, o_own, o_far, stat_ref, vt_ref, s_ref,
    *, scale
):
    holders, _, rows, width = kv_ref.shape
    col_keys = holders * rows
    chunks = col_keys // TILE
    per = TILE // rows
    own_tiles = o_own.shape[0]

    for c in range(chunks):
        vals = kv_ref[c * per : (c + 1) * per, 1].reshape(TILE, width)
        vt_ref[:width, c * TILE : (c + 1) * TILE] = flipped(vals).astype(HALF)
    vt_ref[width:] = jnp.ones((vt_ref.shape[0] - width, col_keys), HALF)
    key_of = lax.broadcasted_iota(jnp.int32, (BLOCK, TILE), 0)
    tiles = 2 * own_tiles

    def rows_of(own, far, tile):
        return (own if tile < own_tiles else far)[tile % own_tiles]

    def scores(tile, c):
        keys = kv_ref[c * per : (c + 1) * per, 0].reshape(TILE, width)
        s = dot_nn(keys, rows_of(qt_own, qt_far, tile)) * scale
        parts = []
        for b in range(TILE // BLOCK):
            at = c * (TILE // BLOCK) + b
            seen = key_of <= limit_ref[tile, at : at + 1]
            parts.append(jnp.where(seen, s[b * BLOCK : (b + 1) * BLOCK], NEG_FILL))
        return jnp.concatenate(parts, axis=0)

    def weigh(tile, top):
        put = slice(tile * TILE, (tile + 1) * TILE)
        out = dot_nn(vt_ref[...], p_ref[:, put])
        total, out = out[width : width + 1], out[:width]
        if tile < own_tiles:
            o_own[tile] = out
        else:
            o_far[tile - own_tiles] = out.astype(HALF)
        g = rows_of(gt_own, gt_far, tile).astype(F32)
        delta = jnp.sum(out * g, axis=0, keepdims=True)
        stat_ref[3 * tile : 3 * tile + 3] = jnp.concatenate([top, total, delta], axis=0)
        return total

    first = kv_ref[0, 0, :BLOCK]
    guesses = [
        jnp.max(dot_nn(first, rows_of(qt_own, qt_far, t)) * scale, axis=0, keepdims=True)
        for t in range(tiles)
    ]

    def guessed(tile):
        put = slice(tile * TILE, (tile + 1) * TILE)
        for c in range(chunks):
            p = jnp.exp2(scores(tile, c) - guesses[tile])
            p_ref[c * TILE : (c + 1) * TILE, put] = p.astype(HALF)

    wrong = jnp.zeros((1, TILE), F32)
    guessed(0)
    for tile in range(tiles):
        if tile + 1 < tiles:
            guessed(tile + 1)
        seen = jnp.max(limit_ref[tile], axis=0, keepdims=True) >= 0
        total = weigh(tile, jnp.where(seen, guesses[tile], NEG_FILL))
        fine = jnp.logical_and(total >= 1.0 / WIDEST, total <= WIDEST)
        wrong = jnp.where(jnp.logical_and(seen, jnp.logical_not(fine)), 1.0, wrong)

    @pl.when(jnp.max(wrong) > 0.0)
    def _():
        for tile in range(tiles):
            put = slice(tile * TILE, (tile + 1) * TILE)
            top = jnp.full((1, TILE), NEG_FILL, F32)
            for c in range(chunks):
                s = scores(tile, c)
                s_ref[c * TILE : (c + 1) * TILE] = s
                top = jnp.maximum(top, jnp.max(s, axis=0, keepdims=True))
            for c in range(chunks):
                span = slice(c * TILE, (c + 1) * TILE)
                p_ref[span, put] = jnp.exp2(s_ref[span] - top).astype(HALF)
            weigh(tile, top)


def backward_kernel(
    side_ref, qt_own, qt_far, gt_own, gt_far, kv_ref, p_ref, stat_ref,
    dkv_ref, dq_own, dq_far, factor_ref, qs_ref, gs_ref, ds_ref, kt_ref, done_ref, sems,
    *, scale
):
    holders, _, rows, width = kv_ref.shape
    chunks = holders * rows // TILE
    per = TILE // rows
    own_tiles = gt_own.shape[0]
    tiles = 2 * own_tiles
    flip_keys(kv_ref, kt_ref)
    deltas, factors = [], []
    right = side_ref[0:1] > 0
    for tile in range(tiles):
        mine = tile < own_tiles
        local = tile % own_tiles
        other = (tile + own_tiles) % tiles
        here, there = (
            [jnp.where(right, stat_ref[1 - s, at], stat_ref[s, at]) for at in spans]
            for s, spans in (
                (0, [slice(3 * tile + i, 3 * tile + i + 1) for i in range(3)]),
                (1, [slice(3 * other + i, 3 * other + i + 1) for i in range(3)]),
            )
        )
        top_a, sum_a, delta_a = here
        top_b, sum_b, delta_b = there
        top = jnp.maximum(top_a, top_b)
        fa, fb = jnp.exp2(top_a - top), jnp.exp2(top_b - top)
        inverse = 1.0 / (sum_a * fa + sum_b * fb)
        factor = fa * inverse
        deltas.append((delta_a * fa + delta_b * fb) * inverse)
        factors.append(factor)
        factor_ref[tile, 0:1] = factor
        factor_ref[tile, 1:2] = fb * inverse
        factor_ref[tile, 2:8] = jnp.zeros((6, TILE), F32)
        put = slice(tile * TILE, (tile + 1) * TILE)
        qt = (qt_own if mine else qt_far)[local].astype(F32) * factor
        gt = (gt_own if mine else gt_far)[local].astype(F32) * factor
        qs_ref[put] = qt.T.astype(HALF)
        gs_ref[:, put] = gt.astype(HALF)

    def grads(c):
        span = slice(c * TILE, (c + 1) * TILE)
        vals = kv_ref[c * per : (c + 1) * per, 1].reshape(TILE, width)
        for tile in range(tiles):
            mine = tile < own_tiles
            local = tile % own_tiles
            p = p_ref[span, tile * TILE : (tile + 1) * TILE].astype(F32)
            grad = p * (dot_nn(vals, (gt_own if mine else gt_far)[local]) - deltas[tile])
            ds_ref[span, tile * TILE : (tile + 1) * TILE] = grad.astype(HALF)

    copies = []
    grads(0)
    for c in range(chunks):
        span = slice(c * TILE, (c + 1) * TILE)
        if c + 1 < chunks:
            grads(c + 1)
        dv = dot_nt(gs_ref[...], p_ref[span]).T
        dk = dot_nn(ds_ref[span], qs_ref[...])
        for z in range(per):
            at = c * per + z
            done_ref[at, 0] = (dk[z * rows : (z + 1) * rows] * scale).astype(HALF)
            done_ref[at, 1] = dv[z * rows : (z + 1) * rows].astype(HALF)
            copies.append(pltpu.make_async_copy(done_ref.at[at], dkv_ref.at[at], sems.at[at]))
            copies[-1].start()
    for tile in range(tiles):
        dq = dot_nn(kt_ref[...], ds_ref[:, tile * TILE : (tile + 1) * TILE])
        dq = (dq * (factors[tile] * scale)).astype(HALF)
        (dq_own if tile < own_tiles else dq_far)[tile % own_tiles] = dq
    for copy in copies:
        copy.wait()


def flip_keys(kv_ref, kt_ref):
    holders, _, rows, width = kv_ref.shape
    per = TILE // rows
    for c in range(holders // per):
        keys = kv_ref[c * per : (c + 1) * per, 0].reshape(TILE, width)
        kt_ref[:, c * TILE : (c + 1) * TILE] = flipped(keys).astype(HALF)


def out_kernel(factor_ref, o_own, o_recv, out_ref):
    for t in range(o_own.shape[0]):
        o = o_own[t] * factor_ref[t, 0:1] + o_recv[t].astype(F32) * factor_ref[t, 1:2]
        out_ref[t * TILE : (t + 1) * TILE] = o.T.astype(HALF)


def pack_kernel(dq_ref, out_ref):
    out_ref[...] = dq_ref[...]


def join_kernel(dq_own, dq_recv, out_ref):
    for t in range(dq_own.shape[0]):
        dq = dq_own[t].astype(F32) + dq_recv[t].astype(F32)
        out_ref[t * TILE : (t + 1) * TILE] = dq.T.astype(HALF)


def total_kernel(terms_ref, dk_ref, dv_ref):
    for i, out in enumerate((dk_ref, dv_ref)):
        total = terms_ref[0, i].astype(F32)
        for z in range(1, terms_ref.shape[0]):
            total = total + terms_ref[z, i].astype(F32)
        out[...] = total.astype(HALF)


def call(kernel, name, ins, outs, scratch=(), flops=0, moved=0, exps=0, specs=None, out_specs=None, limit=8):
    return pl.pallas_call(
        kernel,
        in_specs=specs or [VMEM] * len(ins),
        out_specs=out_specs or [VMEM] * len(outs),
        out_shape=[jax.ShapeDtypeStruct(s, d) for s, d in outs],
        scratch_shapes=scratch,
        compiler_params=pltpu.CompilerParams(vmem_limit_bytes=limit * 2**20),
        cost_estimate=pl.CostEstimate(flops=flops, bytes_accessed=moved, transcendentals=exps),
        name=name,
    )(*ins)


def shards(queries, keys, values, output_gradient, block_order):
    tok, heads, width = queries.shape
    ctx_size = lax.axis_size("ctx")
    holders = ctx_size // 2
    columns = [[2 * z + x for z in range(holders)] for x in range(2)]
    swap = [(i, i ^ 1) for i in range(ctx_size)]
    own_rows = tok * heads
    own_tiles = own_rows // TILE
    tiles = 2 * own_tiles
    col_keys = holders * tok
    score_scale = 1.0 / math.sqrt(width)
    product = 2 * own_rows * col_keys * width
    flip_shape = (own_tiles, width, TILE)
    kv_shape = (holders, 2, tok, width)
    flat_shape = (own_rows, width)
    moved = own_rows * width * 8

    q = queries.reshape(flat_shape)
    g = output_gradient.reshape(flat_shape)
    (spread,) = call(
        spread_kernel, "spread", (keys.reshape(tok, width), values.reshape(tok, width)),
        [(kv_shape, HALF)], [pltpu.VMEM((2, tok, width), HALF), pltpu.SemaphoreType.DMA((2 + holders,))],
        moved=2 * col_keys * width, specs=[HBM, HBM], out_specs=[HBM], limit=60,
    )
    kv_all = lax.all_to_all(spread, "ctx", 0, 0, axis_index_groups=columns, tiled=True)
    q_far = lax.ppermute(q, "ctx", swap)
    g_far = lax.ppermute(g, "ctx", swap)
    info = jnp.concatenate([block_order, lax.axis_index("ctx").astype(jnp.int32).reshape(1)])
    pairs = [[2 * z, 2 * z + 1] for z in range(holders)]
    qt_own, gt_own, limits, side = call(
        functools.partial(stage_kernel, repeat=heads), "stage", (info, q, g),
        [
            (flip_shape, HALF),
            (flip_shape, HALF),
            ((tiles, col_keys // BLOCK, TILE), jnp.int32),
            ((8, TILE), jnp.int32),
        ],
        moved=moved, specs=[SMEM, VMEM, VMEM],
    )
    qt_far, gt_far = call(
        flip_kernel, "flip", (q_far, g_far), [(flip_shape, HALF)] * 2, moved=moved
    )

    weights, o_own, o_far, stats = call(
        functools.partial(forward_kernel, scale=score_scale * math.log2(math.e)),
        "forward", (limits, qt_own, qt_far, gt_own, gt_far, kv_all),
        [
            ((col_keys, 2 * own_rows), HALF),
            (flip_shape, F32),
            (flip_shape, HALF),
            ((3 * tiles, TILE), F32),
        ],
        [pltpu.VMEM((width + 16, col_keys), HALF), pltpu.VMEM((col_keys, TILE), F32)],
        flops=4 * product, exps=2 * own_rows * col_keys, limit=12,
    )
    both = lax.all_gather(stats, "ctx", axis_index_groups=pairs)
    o_recv = lax.ppermute(o_far, "ctx", swap)

    dkv, dq_own, dq_far, factors = call(
        functools.partial(backward_kernel, scale=score_scale),
        "backward",
        (side, qt_own, qt_far, gt_own, gt_far, kv_all, weights, both),
        [
            (kv_shape, HALF),
            (flip_shape, HALF),
            (flip_shape, HALF),
            ((tiles, 8, TILE), F32),
        ],
        [
            pltpu.VMEM((2 * own_rows, width), HALF),
            pltpu.VMEM((width, 2 * own_rows), HALF),
            pltpu.VMEM((col_keys, 2 * own_rows), HALF),
            pltpu.VMEM((width, col_keys), HALF),
            pltpu.VMEM(kv_shape, HALF),
            pltpu.SemaphoreType.DMA((holders,)),
        ],
        flops=8 * product, limit=16, out_specs=[HBM, VMEM, VMEM, VMEM],
    )
    terms = lax.all_to_all(dkv, "ctx", 0, 0, axis_index_groups=columns, tiled=True)

    (dq_sent,) = call(
        pack_kernel, "pack", (dq_far,), [(flip_shape, HALF)], moved=own_rows * width * 4
    )
    dq_recv = lax.ppermute(dq_sent, "ctx", swap)
    (attn_out,) = call(
        out_kernel, "out", (factors, o_own, o_recv), [(flat_shape, HALF)], moved=moved
    )
    (grad_queries,) = call(
        join_kernel, "join", (dq_own, dq_recv), [(flat_shape, HALF)], moved=moved
    )
    grad_keys, grad_values = call(
        total_kernel, "total", (terms,), [((tok, width), HALF), ((tok, width), HALF)],
        moved=2 * col_keys * width * 2,
    )
    return (
        attn_out.reshape(tok, heads, width),
        grad_queries.reshape(tok, heads, width),
        grad_keys.reshape(tok, 1, width),
        grad_values.reshape(tok, 1, width),
    )


def solution(mesh):
    tokens = P(("dp", "ctx"), "head", None)
    return jax.shard_map(
        shards,
        mesh=mesh,
        in_specs=(tokens, tokens, tokens, tokens, P("dp")),
        out_specs=(tokens, tokens, tokens, tokens),
        check_vma=False,
    )
```

```python
import functools
import math

import jax
import jax.numpy as jnp
from jax import lax
from jax.experimental import pallas as pl
from jax.experimental.pallas import tpu as pltpu
from jax.sharding import PartitionSpec as P

NEG_FILL = -1e30
WIDEST = 2.0**40
TILE = 256
BLOCK = 64
VMEM = pl.BlockSpec(memory_space=pltpu.VMEM)
SMEM = pl.BlockSpec(memory_space=pltpu.SMEM)
HBM = pl.BlockSpec(memory_space=pltpu.HBM)
F32 = jnp.float32
HALF = jnp.bfloat16


def dot_nt(a, b):
    return lax.dot_general(a, b, (((1,), (1,)), ((), ())), preferred_element_type=F32)


def dot_nn(a, b):
    return lax.dot_general(a, b, (((1,), (0,)), ((), ())), preferred_element_type=F32)


def flipped(a):
    return a.astype(F32).T


def spread_kernel(k_ref, v_ref, out_ref, held, sems):
    loads = [
        pltpu.make_async_copy(ref, held.at[i], sems.at[i]) for i, ref in enumerate((k_ref, v_ref))
    ]
    for load in loads:
        load.start()
    for load in loads:
        load.wait()
    stores = [
        pltpu.make_async_copy(held, out_ref.at[z], sems.at[2 + z]) for z in range(out_ref.shape[0])
    ]
    for store in stores:
        store.start()
    for store in stores:
        store.wait()


def flip_rows(source, out_ref):
    for t in range(out_ref.shape[0]):
        out_ref[t] = flipped(source[t * TILE : (t + 1) * TILE]).astype(HALF)


def stage_kernel(info_ref, q_ref, g_ref, qt_out, gt_out, limit_ref, side_ref, *, repeat):
    own_tiles = gt_out.shape[0]
    tiles, blocks, _ = limit_ref.shape
    last = info_ref.shape[0] - 1
    ctx = info_ref[last]
    side = ctx % 2
    blocks_here = own_tiles * TILE // repeat // BLOCK
    flip_rows(q_ref, qt_out)
    flip_rows(g_ref, gt_out)
    token_of = lax.broadcasted_iota(jnp.int32, (1, TILE), 1) // repeat
    for t in range(tiles):
        device = ctx if t < own_tiles else ctx + 1 - 2 * side
        token = (t % own_tiles) * (TILE // repeat)
        place = info_ref[device * blocks_here + token // BLOCK] * BLOCK + token % BLOCK
        for b in range(blocks):
            stored = ((b // blocks_here) * 2 + side) * blocks_here + b % blocks_here
            limit_ref[t, b : b + 1] = token_of + (place - info_ref[stored] * BLOCK)
    side_ref[...] = jnp.zeros(side_ref.shape, jnp.int32) + side


def flip_kernel(q_ref, g_ref, qt_out, gt_out):
    flip_rows(q_ref, qt_out)
    flip_rows(g_ref, gt_out)


def forward_kernel(
    limit_ref, qt_own, qt_far, gt_own, gt_far, kv_ref, p_ref, o_own, o_far, stat_ref, vt_ref, s_ref,
    *, repeat, scale
):
    holders, _, rows, width = kv_ref.shape
    col_keys = holders * rows
    chunks = col_keys // TILE
    per = TILE // rows
    own_tiles = o_own.shape[0]

    for c in range(chunks):
        vals = kv_ref[c * per : (c + 1) * per, 1].reshape(TILE, width)
        vt_ref[:width, c * TILE : (c + 1) * TILE] = flipped(vals).astype(HALF)
    vt_ref[width:] = jnp.ones((vt_ref.shape[0] - width, col_keys), HALF)
    key_of = lax.broadcasted_iota(jnp.int32, (BLOCK, TILE), 0)
    tiles = 2 * own_tiles

    def rows_of(own, far, tile):
        return (own if tile < own_tiles else far)[tile % own_tiles]

    def scores(tile, c):
        keys = kv_ref[c * per : (c + 1) * per, 0].reshape(TILE, width)
        s = dot_nn(keys, rows_of(qt_own, qt_far, tile)) * scale
        parts = []
        for b in range(TILE // BLOCK):
            at = c * (TILE // BLOCK) + b
            seen = key_of <= limit_ref[tile, at : at + 1]
            parts.append(jnp.where(seen, s[b * BLOCK : (b + 1) * BLOCK], NEG_FILL))
        return jnp.concatenate(parts, axis=0)

    def weigh(tile, top):
        put = slice(tile * TILE, (tile + 1) * TILE)
        out = dot_nn(vt_ref[...], p_ref[:, put])
        total, out = out[width : width + 1], out[:width]
        if tile < own_tiles:
            o_own[tile] = out
        else:
            o_far[tile - own_tiles] = out.astype(HALF)
        g = rows_of(gt_own, gt_far, tile).astype(F32)
        delta = jnp.sum(out * g, axis=0, keepdims=True)
        stat_ref[3 * tile : 3 * tile + 3] = jnp.concatenate([top, total, delta], axis=0)
        return total

    first = kv_ref[0, 0, :BLOCK]
    guesses = [
        jnp.max(dot_nn(first, rows_of(qt_own, qt_far, t)) * scale, axis=0, keepdims=True)
        for t in range(tiles)
    ]

    def guessed(tile):
        put = slice(tile * TILE, (tile + 1) * TILE)
        own_block = tile * (TILE // repeat) // BLOCK if tile < own_tiles else None
        for c in range(chunks):
            keys = kv_ref[c * per : (c + 1) * per, 0].reshape(TILE, width)
            s = dot_nn(keys, rows_of(qt_own, qt_far, tile)) * scale
            parts = []
            for b in range(TILE // BLOCK):
                at = c * (TILE // BLOCK) + b
                part = s[b * BLOCK : (b + 1) * BLOCK]
                limit = limit_ref[tile, at : at + 1]
                if at % (rows // BLOCK) == own_block:
                    part = jnp.where(key_of <= limit, part, NEG_FILL)
                parts.append(part - jnp.where(limit >= 0, guesses[tile], -NEG_FILL))
            p = jnp.exp2(jnp.concatenate(parts, axis=0))
            p_ref[c * TILE : (c + 1) * TILE, put] = p.astype(HALF)

    wrong = jnp.zeros((1, TILE), F32)
    guessed(0)
    for tile in range(tiles):
        if tile + 1 < tiles:
            guessed(tile + 1)
        seen = jnp.max(limit_ref[tile], axis=0, keepdims=True) >= 0
        total = weigh(tile, jnp.where(seen, guesses[tile], NEG_FILL))
        fine = jnp.logical_and(total >= 1.0 / WIDEST, total <= WIDEST)
        wrong = jnp.where(jnp.logical_and(seen, jnp.logical_not(fine)), 1.0, wrong)

    @pl.when(jnp.max(wrong) > 0.0)
    def _():
        for tile in range(tiles):
            put = slice(tile * TILE, (tile + 1) * TILE)
            top = jnp.full((1, TILE), NEG_FILL, F32)
            for c in range(chunks):
                s = scores(tile, c)
                s_ref[c * TILE : (c + 1) * TILE] = s
                top = jnp.maximum(top, jnp.max(s, axis=0, keepdims=True))
            for c in range(chunks):
                span = slice(c * TILE, (c + 1) * TILE)
                p_ref[span, put] = jnp.exp2(s_ref[span] - top).astype(HALF)
            weigh(tile, top)


def backward_kernel(
    side_ref, qt_own, qt_far, gt_own, gt_far, kv_ref, p_ref, stat_ref,
    dkv_ref, dq_own, dq_far, factor_ref, qs_ref, gs_ref, ds_ref, kt_ref, done_ref, sems,
    *, scale
):
    holders, _, rows, width = kv_ref.shape
    chunks = holders * rows // TILE
    per = TILE // rows
    own_tiles = gt_own.shape[0]
    tiles = 2 * own_tiles
    flip_keys(kv_ref, kt_ref)
    deltas, factors = [], []
    right = side_ref[0:1] > 0
    for tile in range(tiles):
        mine = tile < own_tiles
        local = tile % own_tiles
        other = (tile + own_tiles) % tiles
        here, there = (
            [jnp.where(right, stat_ref[1 - s, at], stat_ref[s, at]) for at in spans]
            for s, spans in (
                (0, [slice(3 * tile + i, 3 * tile + i + 1) for i in range(3)]),
                (1, [slice(3 * other + i, 3 * other + i + 1) for i in range(3)]),
            )
        )
        top_a, sum_a, delta_a = here
        top_b, sum_b, delta_b = there
        top = jnp.maximum(top_a, top_b)
        fa, fb = jnp.exp2(top_a - top), jnp.exp2(top_b - top)
        inverse = 1.0 / (sum_a * fa + sum_b * fb)
        factor = fa * inverse
        deltas.append((delta_a * fa + delta_b * fb) * inverse)
        factors.append(factor)
        factor_ref[tile, 0:1] = factor
        factor_ref[tile, 1:2] = fb * inverse
        factor_ref[tile, 2:8] = jnp.zeros((6, TILE), F32)
        put = slice(tile * TILE, (tile + 1) * TILE)
        qt = (qt_own if mine else qt_far)[local].astype(F32) * factor
        gt = (gt_own if mine else gt_far)[local].astype(F32) * factor
        qs_ref[put] = qt.T.astype(HALF)
        gs_ref[:, put] = gt.astype(HALF)

    def grads(c):
        span = slice(c * TILE, (c + 1) * TILE)
        vals = kv_ref[c * per : (c + 1) * per, 1].reshape(TILE, width)
        for tile in range(tiles):
            mine = tile < own_tiles
            local = tile % own_tiles
            p = p_ref[span, tile * TILE : (tile + 1) * TILE].astype(F32)
            grad = p * (dot_nn(vals, (gt_own if mine else gt_far)[local]) - deltas[tile])
            ds_ref[span, tile * TILE : (tile + 1) * TILE] = grad.astype(HALF)

    copies = []
    grads(0)
    for c in range(chunks):
        span = slice(c * TILE, (c + 1) * TILE)
        if c + 1 < chunks:
            grads(c + 1)
        dv = dot_nt(gs_ref[...], p_ref[span]).T
        dk = dot_nn(ds_ref[span], qs_ref[...])
        for z in range(per):
            at = c * per + z
            done_ref[at, 0] = (dk[z * rows : (z + 1) * rows] * scale).astype(HALF)
            done_ref[at, 1] = dv[z * rows : (z + 1) * rows].astype(HALF)
            copies.append(pltpu.make_async_copy(done_ref.at[at], dkv_ref.at[at], sems.at[at]))
            copies[-1].start()
    for tile in range(tiles):
        dq = dot_nn(kt_ref[...], ds_ref[:, tile * TILE : (tile + 1) * TILE])
        dq = (dq * (factors[tile] * scale)).astype(HALF)
        (dq_own if tile < own_tiles else dq_far)[tile % own_tiles] = dq
    for copy in copies:
        copy.wait()


def flip_keys(kv_ref, kt_ref):
    holders, _, rows, width = kv_ref.shape
    per = TILE // rows
    for c in range(holders // per):
        keys = kv_ref[c * per : (c + 1) * per, 0].reshape(TILE, width)
        kt_ref[:, c * TILE : (c + 1) * TILE] = flipped(keys).astype(HALF)


def out_kernel(factor_ref, o_own, o_recv, out_ref):
    for t in range(o_own.shape[0]):
        o = o_own[t] * factor_ref[t, 0:1] + o_recv[t].astype(F32) * factor_ref[t, 1:2]
        out_ref[t * TILE : (t + 1) * TILE] = o.T.astype(HALF)


def pack_kernel(dq_ref, out_ref):
    out_ref[...] = dq_ref[...]


def join_kernel(dq_own, dq_recv, out_ref):
    for t in range(dq_own.shape[0]):
        dq = dq_own[t].astype(F32) + dq_recv[t].astype(F32)
        out_ref[t * TILE : (t + 1) * TILE] = dq.T.astype(HALF)


def total_kernel(terms_ref, dk_ref, dv_ref):
    for i, out in enumerate((dk_ref, dv_ref)):
        total = terms_ref[0, i].astype(F32)
        for z in range(1, terms_ref.shape[0]):
            total = total + terms_ref[z, i].astype(F32)
        out[...] = total.astype(HALF)


def call(kernel, name, ins, outs, scratch=(), flops=0, moved=0, exps=0, specs=None, out_specs=None, limit=8):
    return pl.pallas_call(
        kernel,
        in_specs=specs or [VMEM] * len(ins),
        out_specs=out_specs or [VMEM] * len(outs),
        out_shape=[jax.ShapeDtypeStruct(s, d) for s, d in outs],
        scratch_shapes=scratch,
        compiler_params=pltpu.CompilerParams(vmem_limit_bytes=limit * 2**20),
        cost_estimate=pl.CostEstimate(flops=flops, bytes_accessed=moved, transcendentals=exps),
        name=name,
    )(*ins)


def shards(queries, keys, values, output_gradient, block_order):
    tok, heads, width = queries.shape
    ctx_size = lax.axis_size("ctx")
    holders = ctx_size // 2
    columns = [[2 * z + x for z in range(holders)] for x in range(2)]
    swap = [(i, i ^ 1) for i in range(ctx_size)]
    own_rows = tok * heads
    own_tiles = own_rows // TILE
    tiles = 2 * own_tiles
    col_keys = holders * tok
    score_scale = 1.0 / math.sqrt(width)
    product = 2 * own_rows * col_keys * width
    flip_shape = (own_tiles, width, TILE)
    kv_shape = (holders, 2, tok, width)
    flat_shape = (own_rows, width)
    moved = own_rows * width * 8

    q = queries.reshape(flat_shape)
    g = output_gradient.reshape(flat_shape)
    (spread,) = call(
        spread_kernel, "spread", (keys.reshape(tok, width), values.reshape(tok, width)),
        [(kv_shape, HALF)], [pltpu.VMEM((2, tok, width), HALF), pltpu.SemaphoreType.DMA((2 + holders,))],
        moved=2 * col_keys * width, specs=[HBM, HBM], out_specs=[HBM], limit=60,
    )
    kv_all = lax.all_to_all(spread, "ctx", 0, 0, axis_index_groups=columns, tiled=True)
    q_far = lax.ppermute(q, "ctx", swap)
    g_far = lax.ppermute(g, "ctx", swap)
    info = jnp.concatenate([block_order, lax.axis_index("ctx").astype(jnp.int32).reshape(1)])
    pairs = [[2 * z, 2 * z + 1] for z in range(holders)]
    qt_own, gt_own, limits, side = call(
        functools.partial(stage_kernel, repeat=heads), "stage", (info, q, g),
        [
            (flip_shape, HALF),
            (flip_shape, HALF),
            ((tiles, col_keys // BLOCK, TILE), jnp.int32),
            ((8, TILE), jnp.int32),
        ],
        moved=moved, specs=[SMEM, VMEM, VMEM],
    )
    qt_far, gt_far = call(
        flip_kernel, "flip", (q_far, g_far), [(flip_shape, HALF)] * 2, moved=moved
    )

    weights, o_own, o_far, stats = call(
        functools.partial(
            forward_kernel, repeat=heads, scale=score_scale * math.log2(math.e)
        ),
        "forward", (limits, qt_own, qt_far, gt_own, gt_far, kv_all),
        [
            ((col_keys, 2 * own_rows), HALF),
            (flip_shape, F32),
            (flip_shape, HALF),
            ((3 * tiles, TILE), F32),
        ],
        [pltpu.VMEM((width + 16, col_keys), HALF), pltpu.VMEM((col_keys, TILE), F32)],
        flops=4 * product, exps=2 * own_rows * col_keys, limit=12,
    )
    both = lax.all_gather(stats, "ctx", axis_index_groups=pairs)
    o_recv = lax.ppermute(o_far, "ctx", swap)

    dkv, dq_own, dq_far, factors = call(
        functools.partial(backward_kernel, scale=score_scale),
        "backward",
        (side, qt_own, qt_far, gt_own, gt_far, kv_all, weights, both),
        [
            (kv_shape, HALF),
            (flip_shape, HALF),
            (flip_shape, HALF),
            ((tiles, 8, TILE), F32),
        ],
        [
            pltpu.VMEM((2 * own_rows, width), HALF),
            pltpu.VMEM((width, 2 * own_rows), HALF),
            pltpu.VMEM((col_keys, 2 * own_rows), HALF),
            pltpu.VMEM((width, col_keys), HALF),
            pltpu.VMEM(kv_shape, HALF),
            pltpu.SemaphoreType.DMA((holders,)),
        ],
        flops=8 * product, limit=16, out_specs=[HBM, VMEM, VMEM, VMEM],
    )
    terms = lax.all_to_all(dkv, "ctx", 0, 0, axis_index_groups=columns, tiled=True)

    (dq_sent,) = call(
        pack_kernel, "pack", (dq_far,), [(flip_shape, HALF)], moved=own_rows * width * 4
    )
    dq_recv = lax.ppermute(dq_sent, "ctx", swap)
    (attn_out,) = call(
        out_kernel, "out", (factors, o_own, o_recv), [(flat_shape, HALF)], moved=moved
    )
    (grad_queries,) = call(
        join_kernel, "join", (dq_own, dq_recv), [(flat_shape, HALF)], moved=moved
    )
    grad_keys, grad_values = call(
        total_kernel, "total", (terms,), [((tok, width), HALF), ((tok, width), HALF)],
        moved=2 * col_keys * width * 2,
    )
    return (
        attn_out.reshape(tok, heads, width),
        grad_queries.reshape(tok, heads, width),
        grad_keys.reshape(tok, 1, width),
        grad_values.reshape(tok, 1, width),
    )


def solution(mesh):
    tokens = P(("dp", "ctx"), "head", None)
    return jax.shard_map(
        shards,
        mesh=mesh,
        in_specs=(tokens, tokens, tokens, tokens, P("dp")),
        out_specs=(tokens, tokens, tokens, tokens),
        check_vma=False,
    )
```

```python
import functools
import math

import jax
import jax.numpy as jnp
from jax import lax
from jax.experimental import pallas as pl
from jax.experimental.pallas import tpu as pltpu
from jax.sharding import PartitionSpec as P

NEG_FILL = -1e30
WIDEST = 2.0**40
TILE = 256
BLOCK = 64
VMEM = pl.BlockSpec(memory_space=pltpu.VMEM)
SMEM = pl.BlockSpec(memory_space=pltpu.SMEM)
HBM = pl.BlockSpec(memory_space=pltpu.HBM)
F32 = jnp.float32
HALF = jnp.bfloat16


def dot_nt(a, b):
    return lax.dot_general(a, b, (((1,), (1,)), ((), ())), preferred_element_type=F32)


def dot_nn(a, b):
    return lax.dot_general(a, b, (((1,), (0,)), ((), ())), preferred_element_type=F32)


def flipped(a):
    return a.astype(F32).T


def spread_kernel(k_ref, v_ref, out_ref, held, sems):
    loads = [
        pltpu.make_async_copy(ref, held.at[i], sems.at[i]) for i, ref in enumerate((k_ref, v_ref))
    ]
    for load in loads:
        load.start()
    for load in loads:
        load.wait()
    stores = [
        pltpu.make_async_copy(held, out_ref.at[z], sems.at[2 + z]) for z in range(out_ref.shape[0])
    ]
    for store in stores:
        store.start()
    for store in stores:
        store.wait()


def flip_rows(source, out_ref):
    for t in range(out_ref.shape[0]):
        out_ref[t] = flipped(source[t * TILE : (t + 1) * TILE]).astype(HALF)


def stage_kernel(info_ref, q_ref, g_ref, qt_out, gt_out, limit_ref, *, repeat):
    own_tiles = gt_out.shape[0]
    tiles, blocks, _ = limit_ref.shape
    last = info_ref.shape[0] - 1
    ctx = info_ref[last]
    side = ctx % 2
    blocks_here = own_tiles * TILE // repeat // BLOCK
    flip_rows(q_ref, qt_out)
    flip_rows(g_ref, gt_out)
    token_of = lax.broadcasted_iota(jnp.int32, (1, TILE), 1) // repeat
    for t in range(tiles):
        device = ctx if t < own_tiles else ctx + 1 - 2 * side
        token = (t % own_tiles) * (TILE // repeat)
        place = info_ref[device * blocks_here + token // BLOCK] * BLOCK + token % BLOCK
        for b in range(blocks):
            stored = ((b // blocks_here) * 2 + side) * blocks_here + b % blocks_here
            limit_ref[t, b : b + 1] = token_of + (place - info_ref[stored] * BLOCK)


def flip_kernel(q_ref, g_ref, qt_out, gt_out):
    flip_rows(q_ref, qt_out)
    flip_rows(g_ref, gt_out)


def forward_kernel(
    limit_ref, qt_own, qt_far, gt_own, gt_far, kv_ref, p_ref, o_own, o_far, stat_ref, vt_ref, s_ref,
    *, repeat, scale
):
    holders, _, rows, width = kv_ref.shape
    col_keys = holders * rows
    chunks = col_keys // TILE
    per = TILE // rows
    own_tiles = o_own.shape[0]

    for c in range(chunks):
        vals = kv_ref[c * per : (c + 1) * per, 1].reshape(TILE, width)
        vt_ref[:width, c * TILE : (c + 1) * TILE] = flipped(vals).astype(HALF)
    vt_ref[width:] = jnp.ones((vt_ref.shape[0] - width, col_keys), HALF)
    key_of = lax.broadcasted_iota(jnp.int32, (BLOCK, TILE), 0)
    tiles = 2 * own_tiles

    def rows_of(own, far, tile):
        return (own if tile < own_tiles else far)[tile % own_tiles]

    def scores(tile, c):
        keys = kv_ref[c * per : (c + 1) * per, 0].reshape(TILE, width)
        s = dot_nn(keys, rows_of(qt_own, qt_far, tile)) * scale
        parts = []
        for b in range(TILE // BLOCK):
            at = c * (TILE // BLOCK) + b
            seen = key_of <= limit_ref[tile, at : at + 1]
            parts.append(jnp.where(seen, s[b * BLOCK : (b + 1) * BLOCK], NEG_FILL))
        return jnp.concatenate(parts, axis=0)

    def weigh(tile, top):
        put = slice(tile * TILE, (tile + 1) * TILE)
        out = dot_nn(vt_ref[...], p_ref[:, put])
        total, out = out[width : width + 1], out[:width]
        if tile < own_tiles:
            o_own[tile] = out
        else:
            o_far[tile - own_tiles] = out.astype(HALF)
        g = rows_of(gt_own, gt_far, tile).astype(F32)
        delta = jnp.sum(out * g, axis=0, keepdims=True)
        stat_ref[3 * tile : 3 * tile + 3] = jnp.concatenate([top, total, delta], axis=0)
        return total

    first = kv_ref[0, 0, :BLOCK]
    guesses = [
        jnp.max(dot_nn(first, rows_of(qt_own, qt_far, t)) * scale, axis=0, keepdims=True)
        for t in range(tiles)
    ]

    def guessed(tile):
        put = slice(tile * TILE, (tile + 1) * TILE)
        own_block = tile * (TILE // repeat) // BLOCK if tile < own_tiles else None
        for c in range(chunks):
            keys = kv_ref[c * per : (c + 1) * per, 0].reshape(TILE, width)
            s = dot_nn(keys, rows_of(qt_own, qt_far, tile)) * scale
            parts = []
            for b in range(TILE // BLOCK):
                at = c * (TILE // BLOCK) + b
                part = s[b * BLOCK : (b + 1) * BLOCK]
                limit = limit_ref[tile, at : at + 1]
                if at % (rows // BLOCK) == own_block:
                    part = jnp.where(key_of <= limit, part, NEG_FILL)
                parts.append(part - jnp.where(limit >= 0, guesses[tile], -NEG_FILL))
            p = jnp.exp2(jnp.concatenate(parts, axis=0))
            if tile == tiles - 1:
                sums.append(jnp.sum(p.reshape(TILE // 8, 8, TILE), axis=0))
            p_ref[c * TILE : (c + 1) * TILE, put] = p.astype(HALF)

    def bad(seen, total):
        fine = jnp.logical_and(total >= 1.0 / WIDEST, total <= WIDEST)
        return jnp.where(jnp.logical_and(seen, jnp.logical_not(fine)), 1.0, 0.0)

    wrong = jnp.zeros((1, TILE), F32)
    sums = []
    guessed(0)
    for tile in range(tiles):
        if tile + 1 < tiles:
            guessed(tile + 1)
        seen = jnp.max(limit_ref[tile], axis=0, keepdims=True) >= 0
        if tile == tiles - 1:
            total = jnp.sum(sum(sums[1:], sums[0]), axis=0, keepdims=True)
            again = jnp.max(jnp.maximum(wrong, bad(seen, total))) > 0.0
        total = weigh(tile, jnp.where(seen, guesses[tile], NEG_FILL))
        wrong = jnp.maximum(wrong, bad(seen, total))

    @pl.when(again)
    def _():
        for tile in range(tiles):
            put = slice(tile * TILE, (tile + 1) * TILE)
            top = jnp.full((1, TILE), NEG_FILL, F32)
            for c in range(chunks):
                s = scores(tile, c)
                s_ref[c * TILE : (c + 1) * TILE] = s
                top = jnp.maximum(top, jnp.max(s, axis=0, keepdims=True))
            for c in range(chunks):
                span = slice(c * TILE, (c + 1) * TILE)
                p_ref[span, put] = jnp.exp2(s_ref[span] - top).astype(HALF)
            weigh(tile, top)


def middle_kernel(gt_own, gt_far, kv_ref, dp_ref):
    holders, _, rows, width = kv_ref.shape
    per = TILE // rows
    own_tiles = gt_own.shape[0]
    for c in range(holders // per):
        vals = kv_ref[c * per : (c + 1) * per, 1].reshape(TILE, width)
        for tile in range(2 * own_tiles):
            gt = (gt_own if tile < own_tiles else gt_far)[tile % own_tiles]
            span = slice(tile * TILE, (tile + 1) * TILE)
            dp_ref[c * TILE : (c + 1) * TILE, span] = dot_nn(vals, gt)


def backward_kernel(
    qt_own, qt_far, gt_own, gt_far, kv_ref, p_ref, dp_ref, here_ref, there_ref,
    dkv_ref, dq_own, dq_far, factor_ref, qs_ref, gs_ref, ds_ref, kt_ref, done_ref, sems,
    *, scale
):
    holders, _, rows, width = kv_ref.shape
    chunks = holders * rows // TILE
    per = TILE // rows
    own_tiles = gt_own.shape[0]
    tiles = 2 * own_tiles
    flip_keys(kv_ref, kt_ref)
    deltas, factors = [], []
    for tile in range(tiles):
        mine = tile < own_tiles
        local = tile % own_tiles
        other = (tile + own_tiles) % tiles
        top_a, sum_a, delta_a = (here_ref[3 * tile + i : 3 * tile + i + 1] for i in range(3))
        top_b, sum_b, delta_b = (there_ref[3 * other + i : 3 * other + i + 1] for i in range(3))
        top = jnp.maximum(top_a, top_b)
        fa, fb = jnp.exp2(top_a - top), jnp.exp2(top_b - top)
        inverse = 1.0 / (sum_a * fa + sum_b * fb)
        factor = fa * inverse
        deltas.append((delta_a * fa + delta_b * fb) * inverse)
        factors.append(factor)
        factor_ref[tile, 0:1] = factor
        factor_ref[tile, 1:2] = fb * inverse
        factor_ref[tile, 2:8] = jnp.zeros((6, TILE), F32)
        put = slice(tile * TILE, (tile + 1) * TILE)
        qt = (qt_own if mine else qt_far)[local].astype(F32) * factor
        gt = (gt_own if mine else gt_far)[local].astype(F32) * factor
        qs_ref[put] = qt.T.astype(HALF)
        gs_ref[:, put] = gt.astype(HALF)

    def grads(c):
        span = slice(c * TILE, (c + 1) * TILE)
        for tile in range(tiles):
            put = slice(tile * TILE, (tile + 1) * TILE)
            grad = p_ref[span, put].astype(F32) * (dp_ref[span, put] - deltas[tile])
            ds_ref[span, put] = grad.astype(HALF)

    copies = []
    grads(0)
    for c in range(chunks):
        span = slice(c * TILE, (c + 1) * TILE)
        if c + 1 < chunks:
            grads(c + 1)
        dv = dot_nt(gs_ref[...], p_ref[span]).T
        dk = dot_nn(ds_ref[span], qs_ref[...])
        for z in range(per):
            at = c * per + z
            done_ref[at, 0] = (dk[z * rows : (z + 1) * rows] * scale).astype(HALF)
            done_ref[at, 1] = dv[z * rows : (z + 1) * rows].astype(HALF)
            copies.append(pltpu.make_async_copy(done_ref.at[at], dkv_ref.at[at], sems.at[at]))
            copies[-1].start()
    for tile in range(tiles):
        dq = dot_nn(kt_ref[...], ds_ref[:, tile * TILE : (tile + 1) * TILE])
        dq = (dq * (factors[tile] * scale)).astype(HALF)
        (dq_own if tile < own_tiles else dq_far)[tile % own_tiles] = dq
    for copy in copies:
        copy.wait()


def flip_keys(kv_ref, kt_ref):
    holders, _, rows, width = kv_ref.shape
    per = TILE // rows
    for c in range(holders // per):
        keys = kv_ref[c * per : (c + 1) * per, 0].reshape(TILE, width)
        kt_ref[:, c * TILE : (c + 1) * TILE] = flipped(keys).astype(HALF)


def out_kernel(factor_ref, o_own, o_recv, out_ref):
    for t in range(o_own.shape[0]):
        o = o_own[t] * factor_ref[t, 0:1] + o_recv[t].astype(F32) * factor_ref[t, 1:2]
        out_ref[t * TILE : (t + 1) * TILE] = o.T.astype(HALF)


def pack_kernel(dq_ref, out_ref):
    out_ref[...] = dq_ref[...]


def join_kernel(dq_own, dq_recv, out_ref):
    for t in range(dq_own.shape[0]):
        dq = dq_own[t].astype(F32) + dq_recv[t].astype(F32)
        out_ref[t * TILE : (t + 1) * TILE] = dq.T.astype(HALF)


def total_kernel(terms_ref, dk_ref, dv_ref):
    for i, out in enumerate((dk_ref, dv_ref)):
        total = terms_ref[0, i].astype(F32)
        for z in range(1, terms_ref.shape[0]):
            total = total + terms_ref[z, i].astype(F32)
        out[...] = total.astype(HALF)


def call(kernel, name, ins, outs, scratch=(), flops=0, moved=0, exps=0, specs=None, out_specs=None, limit=8):
    return pl.pallas_call(
        kernel,
        in_specs=specs or [VMEM] * len(ins),
        out_specs=out_specs or [VMEM] * len(outs),
        out_shape=[jax.ShapeDtypeStruct(s, d) for s, d in outs],
        scratch_shapes=scratch,
        compiler_params=pltpu.CompilerParams(vmem_limit_bytes=limit * 2**20),
        cost_estimate=pl.CostEstimate(flops=flops, bytes_accessed=moved, transcendentals=exps),
        name=name,
    )(*ins)


def shards(queries, keys, values, output_gradient, block_order):
    tok, heads, width = queries.shape
    ctx_size = lax.axis_size("ctx")
    holders = ctx_size // 2
    columns = [[2 * z + x for z in range(holders)] for x in range(2)]
    swap = [(i, i ^ 1) for i in range(ctx_size)]
    own_rows = tok * heads
    own_tiles = own_rows // TILE
    tiles = 2 * own_tiles
    col_keys = holders * tok
    score_scale = 1.0 / math.sqrt(width)
    product = 2 * own_rows * col_keys * width
    flip_shape = (own_tiles, width, TILE)
    kv_shape = (holders, 2, tok, width)
    flat_shape = (own_rows, width)
    moved = own_rows * width * 8

    q = queries.reshape(flat_shape)
    g = output_gradient.reshape(flat_shape)
    (spread,) = call(
        spread_kernel, "spread", (keys.reshape(tok, width), values.reshape(tok, width)),
        [(kv_shape, HALF)], [pltpu.VMEM((2, tok, width), HALF), pltpu.SemaphoreType.DMA((2 + holders,))],
        moved=2 * col_keys * width, specs=[HBM, HBM], out_specs=[HBM], limit=60,
    )
    kv_all = lax.all_to_all(spread, "ctx", 0, 0, axis_index_groups=columns, tiled=True)
    q_far = lax.ppermute(q, "ctx", swap)
    g_far = lax.ppermute(g, "ctx", swap)
    info = jnp.concatenate([block_order, lax.axis_index("ctx").astype(jnp.int32).reshape(1)])
    qt_own, gt_own, limits = call(
        functools.partial(stage_kernel, repeat=heads), "stage", (info, q, g),
        [
            (flip_shape, HALF),
            (flip_shape, HALF),
            ((tiles, col_keys // BLOCK, TILE), jnp.int32),
        ],
        moved=moved, specs=[SMEM, VMEM, VMEM],
    )
    qt_far, gt_far = call(
        flip_kernel, "flip", (q_far, g_far), [(flip_shape, HALF)] * 2, moved=moved
    )

    weights, o_own, o_far, stats = call(
        functools.partial(
            forward_kernel, repeat=heads, scale=score_scale * math.log2(math.e)
        ),
        "forward", (limits, qt_own, qt_far, gt_own, gt_far, kv_all),
        [
            ((col_keys, 2 * own_rows), HALF),
            (flip_shape, F32),
            (flip_shape, HALF),
            ((3 * tiles, TILE), F32),
        ],
        [pltpu.VMEM((width + 16, col_keys), HALF), pltpu.VMEM((col_keys, TILE), F32)],
        flops=4 * product, exps=2 * own_rows * col_keys, limit=12,
    )
    there = lax.ppermute(stats, "ctx", swap)
    (grad_weights,) = call(
        middle_kernel, "middle", (gt_own, gt_far, kv_all),
        [((col_keys, 2 * own_rows), F32)], flops=2 * product, moved=8 * own_rows * col_keys,
    )
    o_recv = lax.ppermute(o_far, "ctx", swap)

    dkv, dq_own, dq_far, factors = call(
        functools.partial(backward_kernel, scale=score_scale),
        "backward",
        (qt_own, qt_far, gt_own, gt_far, kv_all, weights, grad_weights, stats, there),
        [
            (kv_shape, HALF),
            (flip_shape, HALF),
            (flip_shape, HALF),
            ((tiles, 8, TILE), F32),
        ],
        [
            pltpu.VMEM((2 * own_rows, width), HALF),
            pltpu.VMEM((width, 2 * own_rows), HALF),
            pltpu.VMEM((col_keys, 2 * own_rows), HALF),
            pltpu.VMEM((width, col_keys), HALF),
            pltpu.VMEM(kv_shape, HALF),
            pltpu.SemaphoreType.DMA((holders,)),
        ],
        flops=6 * product, limit=16, out_specs=[HBM, VMEM, VMEM, VMEM],
    )
    terms = lax.all_to_all(dkv, "ctx", 0, 0, axis_index_groups=columns, tiled=True)

    (dq_sent,) = call(
        pack_kernel, "pack", (dq_far,), [(flip_shape, HALF)], moved=own_rows * width * 4
    )
    dq_recv = lax.ppermute(dq_sent, "ctx", swap)
    (attn_out,) = call(
        out_kernel, "out", (factors, o_own, o_recv), [(flat_shape, HALF)], moved=moved
    )
    (grad_queries,) = call(
        join_kernel, "join", (dq_own, dq_recv), [(flat_shape, HALF)], moved=moved
    )
    grad_keys, grad_values = call(
        total_kernel, "total", (terms,), [((tok, width), HALF), ((tok, width), HALF)],
        moved=2 * col_keys * width * 2,
    )
    return (
        attn_out.reshape(tok, heads, width),
        grad_queries.reshape(tok, heads, width),
        grad_keys.reshape(tok, 1, width),
        grad_values.reshape(tok, 1, width),
    )


def solution(mesh):
    tokens = P(("dp", "ctx"), "head", None)
    return jax.shard_map(
        shards,
        mesh=mesh,
        in_specs=(tokens, tokens, tokens, tokens, P("dp")),
        out_specs=(tokens, tokens, tokens, tokens),
        check_vma=False,
    )
```

```python
import functools
import math

import jax
import jax.numpy as jnp
from jax import lax
from jax.experimental import pallas as pl
from jax.experimental.pallas import tpu as pltpu
from jax.sharding import PartitionSpec as P

NEG_FILL = -1e30
WIDEST = 2.0**40
TILE = 256
BLOCK = 64
VMEM = pl.BlockSpec(memory_space=pltpu.VMEM)
SMEM = pl.BlockSpec(memory_space=pltpu.SMEM)
HBM = pl.BlockSpec(memory_space=pltpu.HBM)
F32 = jnp.float32
HALF = jnp.bfloat16


def dot_nt(a, b):
    return lax.dot_general(a, b, (((1,), (1,)), ((), ())), preferred_element_type=F32)


def dot_nn(a, b):
    return lax.dot_general(a, b, (((1,), (0,)), ((), ())), preferred_element_type=F32)


def flipped(a):
    return a.astype(F32).T


def spread_kernel(k_ref, v_ref, out_ref, held, sems):
    loads = [
        pltpu.make_async_copy(ref, held.at[i], sems.at[i]) for i, ref in enumerate((k_ref, v_ref))
    ]
    for load in loads:
        load.start()
    for load in loads:
        load.wait()
    stores = [
        pltpu.make_async_copy(held, out_ref.at[z], sems.at[2 + z]) for z in range(out_ref.shape[0])
    ]
    for store in stores:
        store.start()
    for store in stores:
        store.wait()


def flip_rows(source, out_ref):
    for t in range(out_ref.shape[0]):
        out_ref[t] = flipped(source[t * TILE : (t + 1) * TILE]).astype(HALF)


def stage_kernel(info_ref, q_ref, g_ref, qt_out, gt_out, limit_ref, side_ref, *, repeat):
    own_tiles = gt_out.shape[0]
    tiles, blocks, _ = limit_ref.shape
    last = info_ref.shape[0] - 1
    ctx = info_ref[last]
    side = ctx % 2
    blocks_here = own_tiles * TILE // repeat // BLOCK
    flip_rows(q_ref, qt_out)
    flip_rows(g_ref, gt_out)
    token_of = lax.broadcasted_iota(jnp.int32, (1, TILE), 1) // repeat
    for t in range(tiles):
        device = ctx if t < own_tiles else ctx + 1 - 2 * side
        token = (t % own_tiles) * (TILE // repeat)
        place = info_ref[device * blocks_here + token // BLOCK] * BLOCK + token % BLOCK
        for b in range(blocks):
            stored = ((b // blocks_here) * 2 + side) * blocks_here + b % blocks_here
            limit_ref[t, b : b + 1] = token_of + (place - info_ref[stored] * BLOCK)
    side_ref[...] = jnp.zeros(side_ref.shape, jnp.int32) + side


def flip_kernel(q_ref, g_ref, qt_out, gt_out):
    flip_rows(q_ref, qt_out)
    flip_rows(g_ref, gt_out)


def forward_kernel(
    limit_ref, qt_own, qt_far, gt_own, gt_far, kv_ref, p_ref, o_own, o_far, stat_ref, vt_ref, s_ref,
    *, repeat, scale
):
    holders, _, rows, width = kv_ref.shape
    col_keys = holders * rows
    chunks = col_keys // TILE
    per = TILE // rows
    own_tiles = o_own.shape[0]

    for c in range(chunks):
        vals = kv_ref[c * per : (c + 1) * per, 1].reshape(TILE, width)
        vt_ref[:width, c * TILE : (c + 1) * TILE] = flipped(vals).astype(HALF)
    vt_ref[width:] = jnp.ones((vt_ref.shape[0] - width, col_keys), HALF)
    key_of = lax.broadcasted_iota(jnp.int32, (BLOCK, TILE), 0)
    tiles = 2 * own_tiles

    def rows_of(own, far, tile):
        return (own if tile < own_tiles else far)[tile % own_tiles]

    def scores(tile, c):
        keys = kv_ref[c * per : (c + 1) * per, 0].reshape(TILE, width)
        s = dot_nn(keys, rows_of(qt_own, qt_far, tile)) * scale
        parts = []
        for b in range(TILE // BLOCK):
            at = c * (TILE // BLOCK) + b
            seen = key_of <= limit_ref[tile, at : at + 1]
            parts.append(jnp.where(seen, s[b * BLOCK : (b + 1) * BLOCK], NEG_FILL))
        return jnp.concatenate(parts, axis=0)

    def weigh(tile, top):
        put = slice(tile * TILE, (tile + 1) * TILE)
        out = dot_nn(vt_ref[...], p_ref[:, put])
        total, out = out[width : width + 1], out[:width]
        if tile < own_tiles:
            o_own[tile] = out
        else:
            o_far[tile - own_tiles] = out.astype(HALF)
        g = rows_of(gt_own, gt_far, tile).astype(F32)
        delta = jnp.sum(out * g, axis=0, keepdims=True)
        stat_ref[3 * tile : 3 * tile + 3] = jnp.concatenate([top, total, delta], axis=0)
        return total

    first = kv_ref[0, 0, :BLOCK]
    guesses = [
        jnp.max(dot_nn(first, rows_of(qt_own, qt_far, t)) * scale, axis=0, keepdims=True)
        for t in range(tiles)
    ]

    def guessed(tile):
        put = slice(tile * TILE, (tile + 1) * TILE)
        own_block = tile * (TILE // repeat) // BLOCK if tile < own_tiles else None
        for c in range(chunks):
            keys = kv_ref[c * per : (c + 1) * per, 0].reshape(TILE, width)
            s = dot_nn(keys, rows_of(qt_own, qt_far, tile)) * scale
            parts = []
            for b in range(TILE // BLOCK):
                at = c * (TILE // BLOCK) + b
                part = s[b * BLOCK : (b + 1) * BLOCK]
                limit = limit_ref[tile, at : at + 1]
                if at % (rows // BLOCK) == own_block:
                    part = jnp.where(key_of <= limit, part, NEG_FILL)
                parts.append(part - jnp.where(limit >= 0, guesses[tile], -NEG_FILL))
            p = jnp.exp2(jnp.concatenate(parts, axis=0))
            if tile == tiles - 1:
                sums.append(jnp.sum(p.reshape(TILE // 8, 8, TILE), axis=0))
            p_ref[c * TILE : (c + 1) * TILE, put] = p.astype(HALF)

    def bad(seen, total):
        fine = jnp.logical_and(total >= 1.0 / WIDEST, total <= WIDEST)
        return jnp.where(jnp.logical_and(seen, jnp.logical_not(fine)), 1.0, 0.0)

    wrong = jnp.zeros((1, TILE), F32)
    sums = []
    guessed(0)
    for tile in range(tiles):
        if tile + 1 < tiles:
            guessed(tile + 1)
        seen = jnp.max(limit_ref[tile], axis=0, keepdims=True) >= 0
        if tile == tiles - 1:
            total = jnp.sum(sum(sums[1:], sums[0]), axis=0, keepdims=True)
            again = jnp.max(jnp.maximum(wrong, bad(seen, total))) > 0.0
        total = weigh(tile, jnp.where(seen, guesses[tile], NEG_FILL))
        wrong = jnp.maximum(wrong, bad(seen, total))

    @pl.when(again)
    def _():
        for tile in range(tiles):
            put = slice(tile * TILE, (tile + 1) * TILE)
            top = jnp.full((1, TILE), NEG_FILL, F32)
            for c in range(chunks):
                s = scores(tile, c)
                s_ref[c * TILE : (c + 1) * TILE] = s
                top = jnp.maximum(top, jnp.max(s, axis=0, keepdims=True))
            for c in range(chunks):
                span = slice(c * TILE, (c + 1) * TILE)
                p_ref[span, put] = jnp.exp2(s_ref[span] - top).astype(HALF)
            weigh(tile, top)


def backward_kernel(
    side_ref, qt_own, qt_far, gt_own, gt_far, kv_ref, p_ref, stat_ref,
    dkv_ref, dq_own, dq_far, factor_ref, qs_ref, gs_ref, ds_ref, kt_ref, done_ref, sems,
    *, scale
):
    holders, _, rows, width = kv_ref.shape
    chunks = holders * rows // TILE
    per = TILE // rows
    own_tiles = gt_own.shape[0]
    tiles = 2 * own_tiles
    flip_keys(kv_ref, kt_ref)
    deltas, factors = [], []
    right = side_ref[0:1] > 0
    for tile in range(tiles):
        mine = tile < own_tiles
        local = tile % own_tiles
        other = (tile + own_tiles) % tiles
        here, there = (
            [jnp.where(right, stat_ref[1 - s, at], stat_ref[s, at]) for at in spans]
            for s, spans in (
                (0, [slice(3 * tile + i, 3 * tile + i + 1) for i in range(3)]),
                (1, [slice(3 * other + i, 3 * other + i + 1) for i in range(3)]),
            )
        )
        top_a, sum_a, delta_a = here
        top_b, sum_b, delta_b = there
        top = jnp.maximum(top_a, top_b)
        fa, fb = jnp.exp2(top_a - top), jnp.exp2(top_b - top)
        inverse = 1.0 / (sum_a * fa + sum_b * fb)
        factor = fa * inverse
        deltas.append((delta_a * fa + delta_b * fb) * inverse)
        factors.append(factor)
        factor_ref[tile, 0:1] = factor
        factor_ref[tile, 1:2] = fb * inverse
        factor_ref[tile, 2:8] = jnp.zeros((6, TILE), F32)
        put = slice(tile * TILE, (tile + 1) * TILE)
        qt = (qt_own if mine else qt_far)[local].astype(F32) * factor
        gt = (gt_own if mine else gt_far)[local].astype(F32) * factor
        qs_ref[put] = qt.T.astype(HALF)
        gs_ref[:, put] = gt.astype(HALF)

    def grads(c):
        span = slice(c * TILE, (c + 1) * TILE)
        vals = kv_ref[c * per : (c + 1) * per, 1].reshape(TILE, width)
        for tile in range(tiles):
            mine = tile < own_tiles
            local = tile % own_tiles
            p = p_ref[span, tile * TILE : (tile + 1) * TILE].astype(F32)
            grad = p * (dot_nn(vals, (gt_own if mine else gt_far)[local]) - deltas[tile])
            ds_ref[span, tile * TILE : (tile + 1) * TILE] = grad.astype(HALF)

    copies = []
    grads(0)
    for c in range(chunks):
        span = slice(c * TILE, (c + 1) * TILE)
        if c + 1 < chunks:
            grads(c + 1)
        dv = dot_nt(gs_ref[...], p_ref[span]).T
        dk = dot_nn(ds_ref[span], qs_ref[...])
        for z in range(per):
            at = c * per + z
            done_ref[at, 0] = (dk[z * rows : (z + 1) * rows] * scale).astype(HALF)
            done_ref[at, 1] = dv[z * rows : (z + 1) * rows].astype(HALF)
            copies.append(pltpu.make_async_copy(done_ref.at[at], dkv_ref.at[at], sems.at[at]))
            copies[-1].start()
    for tile in range(tiles):
        dq = dot_nn(kt_ref[...], ds_ref[:, tile * TILE : (tile + 1) * TILE])
        dq = (dq * (factors[tile] * scale)).astype(HALF)
        (dq_own if tile < own_tiles else dq_far)[tile % own_tiles] = dq
    for copy in copies:
        copy.wait()


def flip_keys(kv_ref, kt_ref):
    holders, _, rows, width = kv_ref.shape
    per = TILE // rows
    for c in range(holders // per):
        keys = kv_ref[c * per : (c + 1) * per, 0].reshape(TILE, width)
        kt_ref[:, c * TILE : (c + 1) * TILE] = flipped(keys).astype(HALF)


def out_kernel(factor_ref, o_own, o_recv, out_ref):
    for t in range(o_own.shape[0]):
        o = o_own[t] * factor_ref[t, 0:1] + o_recv[t].astype(F32) * factor_ref[t, 1:2]
        out_ref[t * TILE : (t + 1) * TILE] = o.T.astype(HALF)


def pack_kernel(dq_ref, out_ref):
    out_ref[...] = dq_ref[...]


def join_kernel(dq_own, dq_recv, out_ref):
    for t in range(dq_own.shape[0]):
        dq = dq_own[t].astype(F32) + dq_recv[t].astype(F32)
        out_ref[t * TILE : (t + 1) * TILE] = dq.T.astype(HALF)


def total_kernel(terms_ref, dk_ref, dv_ref):
    for i, out in enumerate((dk_ref, dv_ref)):
        total = terms_ref[0, i].astype(F32)
        for z in range(1, terms_ref.shape[0]):
            total = total + terms_ref[z, i].astype(F32)
        out[...] = total.astype(HALF)


def call(kernel, name, ins, outs, scratch=(), flops=0, moved=0, exps=0, specs=None, out_specs=None, limit=8):
    return pl.pallas_call(
        kernel,
        in_specs=specs or [VMEM] * len(ins),
        out_specs=out_specs or [VMEM] * len(outs),
        out_shape=[jax.ShapeDtypeStruct(s, d) for s, d in outs],
        scratch_shapes=scratch,
        compiler_params=pltpu.CompilerParams(vmem_limit_bytes=limit * 2**20),
        cost_estimate=pl.CostEstimate(flops=flops, bytes_accessed=moved, transcendentals=exps),
        name=name,
    )(*ins)


def shards(queries, keys, values, output_gradient, block_order):
    tok, heads, width = queries.shape
    ctx_size = lax.axis_size("ctx")
    holders = ctx_size // 2
    columns = [[2 * z + x for z in range(holders)] for x in range(2)]
    swap = [(i, i ^ 1) for i in range(ctx_size)]
    own_rows = tok * heads
    own_tiles = own_rows // TILE
    tiles = 2 * own_tiles
    col_keys = holders * tok
    score_scale = 1.0 / math.sqrt(width)
    product = 2 * own_rows * col_keys * width
    flip_shape = (own_tiles, width, TILE)
    kv_shape = (holders, 2, tok, width)
    flat_shape = (own_rows, width)
    moved = own_rows * width * 8

    q = queries.reshape(flat_shape)
    g = output_gradient.reshape(flat_shape)
    (spread,) = call(
        spread_kernel, "spread", (keys.reshape(tok, width), values.reshape(tok, width)),
        [(kv_shape, HALF)], [pltpu.VMEM((2, tok, width), HALF), pltpu.SemaphoreType.DMA((2 + holders,))],
        moved=2 * col_keys * width, specs=[HBM, HBM], out_specs=[HBM], limit=60,
    )
    kv_all = lax.all_to_all(spread, "ctx", 0, 0, axis_index_groups=columns, tiled=True)
    q_far = lax.ppermute(q, "ctx", swap)
    g_far = lax.ppermute(g, "ctx", swap)
    info = jnp.concatenate([block_order, lax.axis_index("ctx").astype(jnp.int32).reshape(1)])
    pairs = [[2 * z, 2 * z + 1] for z in range(holders)]
    qt_own, gt_own, limits, side = call(
        functools.partial(stage_kernel, repeat=heads), "stage", (info, q, g),
        [
            (flip_shape, HALF),
            (flip_shape, HALF),
            ((tiles, col_keys // BLOCK, TILE), jnp.int32),
            ((8, TILE), jnp.int32),
        ],
        moved=moved, specs=[SMEM, VMEM, VMEM],
    )
    qt_far, gt_far = call(
        flip_kernel, "flip", (q_far, g_far), [(flip_shape, HALF)] * 2, moved=moved
    )

    weights, o_own, o_far, stats = call(
        functools.partial(
            forward_kernel, repeat=heads, scale=score_scale * math.log2(math.e)
        ),
        "forward", (limits, qt_own, qt_far, gt_own, gt_far, kv_all),
        [
            ((col_keys, 2 * own_rows), HALF),
            (flip_shape, F32),
            (flip_shape, HALF),
            ((3 * tiles, TILE), F32),
        ],
        [pltpu.VMEM((width + 16, col_keys), HALF), pltpu.VMEM((col_keys, TILE), F32)],
        flops=4 * product, exps=2 * own_rows * col_keys, limit=12,
    )
    both = lax.all_gather(stats, "ctx", axis_index_groups=pairs)
    o_recv = lax.ppermute(o_far, "ctx", swap)

    dkv, dq_own, dq_far, factors = call(
        functools.partial(backward_kernel, scale=score_scale),
        "backward",
        (side, qt_own, qt_far, gt_own, gt_far, kv_all, weights, both),
        [
            (kv_shape, HALF),
            (flip_shape, HALF),
            (flip_shape, HALF),
            ((tiles, 8, TILE), F32),
        ],
        [
            pltpu.VMEM((2 * own_rows, width), HALF),
            pltpu.VMEM((width, 2 * own_rows), HALF),
            pltpu.VMEM((col_keys, 2 * own_rows), HALF),
            pltpu.VMEM((width, col_keys), HALF),
            pltpu.VMEM(kv_shape, HALF),
            pltpu.SemaphoreType.DMA((holders,)),
        ],
        flops=8 * product, limit=16, out_specs=[HBM, VMEM, VMEM, VMEM],
    )
    terms = lax.all_to_all(dkv, "ctx", 0, 0, axis_index_groups=columns, tiled=True)

    (dq_sent,) = call(
        pack_kernel, "pack", (dq_far,), [(flip_shape, HALF)], moved=own_rows * width * 4
    )
    dq_recv = lax.ppermute(dq_sent, "ctx", swap)
    (attn_out,) = call(
        out_kernel, "out", (factors, o_own, o_recv), [(flat_shape, HALF)], moved=moved
    )
    (grad_queries,) = call(
        join_kernel, "join", (dq_own, dq_recv), [(flat_shape, HALF)], moved=moved
    )
    grad_keys, grad_values = call(
        total_kernel, "total", (terms,), [((tok, width), HALF), ((tok, width), HALF)],
        moved=2 * col_keys * width * 2,
    )
    return (
        attn_out.reshape(tok, heads, width),
        grad_queries.reshape(tok, heads, width),
        grad_keys.reshape(tok, 1, width),
        grad_values.reshape(tok, 1, width),
    )


def solution(mesh):
    tokens = P(("dp", "ctx"), "head", None)
    return jax.shard_map(
        shards,
        mesh=mesh,
        in_specs=(tokens, tokens, tokens, tokens, P("dp")),
        out_specs=(tokens, tokens, tokens, tokens),
        check_vma=False,
    )
```
